32 devices in a mesh: section: 2 (over core), dp: 16 (over z, y, x).
Axes of the slice: x: 2, y: 2, z: 4, core: 2. Of those that a mesh axis runs over, the one named last changes fastest.
Arguments:
- inputs: bfloat16 [2, 16, 512, 768], P(None, 'dp'), may hold values from -6 to 6, as said below
- cotangent: bfloat16 [2, 16, 512, 768], P(None, 'dp'), may hold values from -6 to 6, as said below
- pair_lengths: int32 [2, 16, 4], P(None, 'dp'), may hold values from 1 to 256, 512 in all within a row
- padding: int32 [2, 16], P(None, 'dp'), may hold values from 0 to 127
- qkv_weights: bfloat16 [2, 3, 768, 768], P('section'), as said below
- out_weights: bfloat16 [2, 768, 768], P('section'), as said below
- up_weights: bfloat16 [2, 768, 3072], P('section'), as said below
- down_weights: bfloat16 [2, 3072, 768], P('section'), as said below
- layer_vectors: float32 [2, 8, 768], P('section'), may hold values from -1.2 to 1.6, as said below
- up_biases: float32 [2, 3072], P('section'), as said below
- shared_in: bfloat16 [1024, 768], replicated, as said below
- shared_out: bfloat16 [768, 1024], replicated, as said below
- scale_rank: float32 [2, 2, 1024], P('section'), may hold values from -4 to 4, as said below
- scale_width: float32 [2, 2, 768], P('section'), may hold values from -2 to 2, as said below
Outputs:
- section_outputs: bfloat16 [2, 2, 16, 512, 768], P('section', None, 'dp')
- input_grads: bfloat16 [2, 2, 16, 512, 768], P('section', None, 'dp')
- grad_rank: float32 [2, 2, 1024], P('section')
- grad_width: float32 [2, 2, 768], P('section')
The draws below stay inside these ranges and needn't reach their ends.
Inputs may be any that keep to these rules, and one draw needn't show every extreme that they name: `layer_vectors`: rows 3 and 6 of each layer are the norms' gains, the other rows biases. `inputs`: entries of mean zero and deviation one. `cotangent`: entries of mean zero and deviation one. `qkv_weights`: entries of mean zero and deviation one over the root of 768, within four deviations. `out_weights`: entries of mean zero and deviation four over the root of 768, within four deviations. `up_weights`: entries of mean zero and deviation one over the root of 768, within four deviations. `down_weights`: entries of mean zero and deviation one over the root of 3072, within four deviations. `up_biases`: entries of mean zero and deviation 0.3. `shared_in`: entries of mean zero and deviation one over the root of 768, within four deviations. `shared_out`: entries of mean zero and deviation one over the root of 1024, within four deviations. `scale_rank`: entries of mean zero and deviation one. `scale_width`: entries of mean zero and deviation 0.5.
All inputs are finite; a program needn't handle non-finite values.
Results may differ from the reference program's by a relative error of at most 0.018.
Values may be sent and summed in bfloat16 or wider, within the bound.
No kernel may reach another device: no remote copies, remote signals or barrier semaphores. Data moves between devices by JAX's collectives and lax.ppermute only.
A program may use at most 256 MiB of HBM per device.

```python
import math
import jax
import jax.numpy as jnp
import numpy as np
from jax import lax

D = 768
HEADS = 12
HEAD_DIM = 64
FF = 3072
RANK = 1024
LEN = 512
PAIRS = 4
MOST = 256
MB = 2
SEQS = 16


def gaussian(key, shape, scale, bound):
    return scale * jnp.clip(jax.random.normal(key, shape, jnp.float32), -bound, bound)


def draw_inputs(key, part):
    key = jax.random.fold_in(key, 21)
    shape = (MB, SEQS, LEN, D)
    return gaussian(key, shape, 1.0, 6.0).astype(jnp.bfloat16)


def draw_cotangent(key, part):
    key = jax.random.fold_in(key, 22)
    shape = (MB, SEQS, LEN, D)
    return gaussian(key, shape, 1.0, 6.0).astype(jnp.bfloat16)


def draw_qkv_weights(key, part):
    key = jax.random.fold_in(key, 23)
    shape = (2, 3, D, D)
    return gaussian(key, shape, D ** (-0.5), 4.0).astype(jnp.bfloat16)


def draw_out_weights(key, part):
    key = jax.random.fold_in(key, 24)
    shape = (2, D, D)
    return gaussian(key, shape, 4.0 * D ** (-0.5), 4.0).astype(jnp.bfloat16)


def draw_up_weights(key, part):
    key = jax.random.fold_in(key, 25)
    shape = (2, D, FF)
    return gaussian(key, shape, D ** (-0.5), 4.0).astype(jnp.bfloat16)


def draw_down_weights(key, part):
    key = jax.random.fold_in(key, 26)
    shape = (2, FF, D)
    return gaussian(key, shape, FF ** (-0.5), 4.0).astype(jnp.bfloat16)


def draw_up_biases(key, part):
    key = jax.random.fold_in(key, 27)
    shape = (2, FF)
    return gaussian(key, shape, 0.3, 5.0).astype(jnp.float32)


def draw_shared_in(key, part):
    key = jax.random.fold_in(key, 28)
    shape = (RANK, D)
    return gaussian(key, shape, D ** (-0.5), 4.0).astype(jnp.bfloat16)


def draw_shared_out(key, part):
    key = jax.random.fold_in(key, 29)
    shape = (D, RANK)
    return gaussian(key, shape, RANK ** (-0.5), 4.0).astype(jnp.bfloat16)


def draw_scale_rank(key, part):
    key = jax.random.fold_in(key, 30)
    shape = (2, 2, RANK)
    return gaussian(key, shape, 1.0, 4.0).astype(jnp.float32)


def draw_scale_width(key, part):
    key = jax.random.fold_in(key, 31)
    shape = (2, 2, D)
    return gaussian(key, shape, 0.5, 4.0).astype(jnp.float32)


def draw_layer_vectors(key, part):
    key = jax.random.fold_in(key, 11)
    normal_draw = jnp.clip(jax.random.normal(key, (2, 8, D), jnp.float32), -4.0, 4.0)
    row_index = jnp.arange(8)[None, :, None]
    gain_rows = (row_index == 3) | (row_index == 6)
    return jnp.where(gain_rows, 1.0 + 0.15 * normal_draw, 0.3 * normal_draw).astype(jnp.float32)


def touch_ends(result, rng, smallest, largest):
    dims = result.shape
    index_at = [jax.random.randint(jax.random.fold_in(rng, axis), (), 0, dims[axis]) for axis in range(len(dims))]
    result = result.at[tuple(index_at)].set(smallest)
    longest = dims.index(max(dims))
    index_at[longest] = (index_at[longest] + 1) % dims[longest]
    return result.at[tuple(index_at)].set(largest)


def split_up(number_of, total, most, lean):
    loads = [(1 << 20) // math.isqrt(grade ** lean) + 1 for grade in range(2, number_of + 1)]
    surplus, given = total - most - (number_of - 1), [1] * (number_of - 1)
    while surplus > 0:
        movable = [i for i in range(number_of - 1) if given[i] < most]
        pool, budget = sum([loads[i] for i in movable]), surplus
        for i in movable:
            addition = min(most - given[i], max(1, budget * loads[i] // pool), surplus)
            given[i] = given[i] + addition
            surplus = surplus - addition
    return np.array([most] + given)


def uneven(stream_key, count, total, most, skew):
    if count == 2:
        one = jax.random.randint(stream_key, (), max(1, total - most), min(most, total - 1) + 1)
        return jnp.stack([one, total - one])
    tallies = jnp.asarray(split_up(count, total, most, skew), jnp.int32)
    pairs = (count - 1) // 2
    giver, taker = tallies[1:1 + 2 * pairs:2], tallies[2:2 + 2 * pairs:2]
    margin = jnp.minimum(giver - 1, most - taker)
    shifted = jax.random.randint(jax.random.fold_in(stream_key, 1), (pairs,), 0, 1 << 20) % (margin + 1)
    tallies = tallies.at[1:1 + 2 * pairs:2].set(giver - shifted).at[2:2 + 2 * pairs:2].set(taker + shifted)
    return tallies[jax.random.permutation(jax.random.fold_in(stream_key, 2), count)]


def setup_inputs(seed: int = 0) -> dict:
    key_list = jax.random.split(jax.random.key(seed), 15)
    inputs = draw_inputs(jax.random.fold_in(key_list[14], 71), 0)
    cotangent = draw_cotangent(jax.random.fold_in(key_list[14], 71), 0)
    pair_lengths = jax.vmap(lambda own: uneven(own, PAIRS, LEN, MOST, 1))(jax.random.split(key_list[2], MB * SEQS)).reshape((MB, SEQS, PAIRS)).astype(jnp.int32)
    padding = touch_ends(jax.random.randint(key_list[3], (MB, SEQS), 0, LEN // 4), jax.random.fold_in(key_list[3], 1), 0, (LEN // 4) - 1).astype(jnp.int32)
    qkv_weights = draw_qkv_weights(jax.random.fold_in(key_list[14], 71), 0)
    out_weights = draw_out_weights(jax.random.fold_in(key_list[14], 71), 0)
    up_weights = draw_up_weights(jax.random.fold_in(key_list[14], 71), 0)
    down_weights = draw_down_weights(jax.random.fold_in(key_list[14], 71), 0)
    layer_vectors = draw_layer_vectors(jax.random.fold_in(key_list[14], 71), 0)
    up_biases = draw_up_biases(jax.random.fold_in(key_list[14], 71), 0)
    shared_in = draw_shared_in(jax.random.fold_in(key_list[14], 71), 0)
    shared_out = draw_shared_out(jax.random.fold_in(key_list[14], 71), 0)
    scale_rank = draw_scale_rank(jax.random.fold_in(key_list[14], 71), 0)
    scale_width = draw_scale_width(jax.random.fold_in(key_list[14], 71), 0)
    return dict(inputs=inputs, cotangent=cotangent, pair_lengths=pair_lengths, padding=padding, qkv_weights=qkv_weights, out_weights=out_weights, up_weights=up_weights, down_weights=down_weights, layer_vectors=layer_vectors, up_biases=up_biases, shared_in=shared_in, shared_out=shared_out, scale_rank=scale_rank, scale_width=scale_width)


@jax.custom_vjp
def low(v):
    return lax.optimization_barrier(v.astype(jnp.bfloat16)).astype(jnp.float32)

@jax.custom_vjp
def low_back(v):
    return v

def low_keep(v):
    return (low(v), None)

def low_pass(kept, grad):
    return (grad,)

def back_keep(v):
    return (v, None)

def back_low(kept, grad):
    return (low(grad),)
low.defvjp(low_keep, low_pass)
low_back.defvjp(back_keep, back_low)
precise = lax.Precision.HIGHEST
epsilon = 1e-05

def product(left, right):
    return jnp.dot(left, right, preferred_element_type=jnp.float32, precision=precise)

def visibility(lengths, pad_count):
    positions = jnp.arange(LEN, dtype=jnp.int32)
    bounds = jnp.cumsum(lengths.astype(jnp.int32)).astype(jnp.int32)
    doc_ids = lax.optimization_barrier(jnp.sum((positions[:, None] >= bounds[None, :]).astype(jnp.int32), axis=1)).astype(jnp.int32)
    live = positions < LEN - pad_count.astype(jnp.int32)
    same = doc_ids[:, None] == doc_ids[None, :]
    return same & live[None, :] | (positions[:, None] == positions[None, :])

def layer_norm(values, gain, shift):
    average = lax.optimization_barrier(jnp.mean(values, axis=-1, keepdims=True))
    centered = values - average
    variance = lax.optimization_barrier(jnp.mean(centered * centered, axis=-1, keepdims=True))
    return centered * lax.rsqrt(variance + epsilon) * gain + shift

def attend(packed):
    queries, key_rows, values, visible = packed
    shaped_q = queries.reshape(LEN, HEADS, HEAD_DIM)
    shaped_k = key_rows.reshape(LEN, HEADS, HEAD_DIM)
    shaped_v = values.reshape(LEN, HEADS, HEAD_DIM)
    scores = jnp.einsum('qhe,khe->hqk', shaped_q, shaped_k, precision=precise) * HEAD_DIM ** (-0.5)
    scores = jnp.where(visible[None], scores, -1e+30)
    scores = low_back(scores)
    weights = jax.nn.softmax(scores, axis=-1)
    context = jnp.einsum('hqk,khe->qhe', low(weights), shaped_v, precision=precise)
    return low_back(low(context.reshape(LEN, D)))

def layer(start, visible, frozen, lower, upper, rank_scale, width_scale):
    qkv, w_out, w_up, w_down, vectors, up_bias = frozen
    hidden = low_back(start)
    reduced = low_back(product(hidden, lower.T))
    rank_q = low(rank_scale[0] * reduced)
    rank_v = low(rank_scale[1] * reduced)
    vera_q = low_back(product(rank_q, upper.T))
    vera_v = low_back(product(rank_v, upper.T))
    queries = low_back(low(product(hidden, qkv[0]) + vectors[0] + width_scale[0] * vera_q))
    key_rows = low_back(low(product(hidden, qkv[1])))
    values = low_back(low(product(hidden, qkv[2]) + vectors[1] + width_scale[1] * vera_v))
    context = lax.map(jax.checkpoint(attend), (queries, key_rows, values, visible))
    attended = low_back(product(context, w_out) + vectors[2])
    first_sum = hidden + attended
    normed = layer_norm(first_sum, vectors[3], vectors[4])
    before = low_back(product(low(normed), w_up) + up_bias)
    activated = low(jax.nn.gelu(before, approximate=False))
    expanded = low_back(product(activated, w_down) + vectors[5])
    return low(layer_norm(normed + expanded, vectors[6], vectors[7]))

def reference(inputs, cotangent, pair_lengths, padding, qkv_weights, out_weights, up_weights, down_weights, layer_vectors, up_biases, shared_in, shared_out, scale_rank, scale_width):
    frozen = [tuple((array[index].astype(jnp.float32) for array in (qkv_weights, out_weights, up_weights, down_weights, layer_vectors, up_biases))) for index in range(2)]
    lower = shared_in.astype(jnp.float32)
    upper = shared_out.astype(jnp.float32)
    rank_scales = scale_rank.astype(jnp.float32)
    width_scales = scale_width.astype(jnp.float32)
    count = MB * SEQS
    group = math.gcd(count, 8)
    batches = count // group
    flat_in = inputs.astype(jnp.float32).reshape(batches, group, LEN, D)
    flat_cot = cotangent.astype(jnp.float32).reshape(batches, group, LEN, D)
    flat_len = pair_lengths.astype(jnp.int32).reshape(batches, group, PAIRS)
    flat_pad = padding.astype(jnp.int32).reshape(batches, group)

    def one_group(carry, item):
        block_in, block_cot, block_len, block_pad = item
        visible = jax.vmap(visibility)(block_len, block_pad)

        def forward(start, probe, rank_vals, width_vals):
            first = layer(start, visible, frozen[0], lower, upper, rank_vals[0], width_vals[0])
            second = layer(first + probe, visible, frozen[1], lower, upper, rank_vals[1], width_vals[1])
            return (first, second)
        outputs, pull = jax.vjp(forward, block_in, jnp.zeros_like(block_in), rank_scales, width_scales)
        grad_start, grad_probe, grad_r, grad_w = pull((jnp.zeros_like(block_in), block_cot))
        return ((carry[0] + grad_r, carry[1] + grad_w), (outputs[0], outputs[1], grad_start, grad_probe))
    sums, stacked = lax.scan(one_group, (jnp.zeros_like(rank_scales), jnp.zeros_like(width_scales)), (flat_in, flat_cot, flat_len, flat_pad))
    section_outputs = jnp.stack([stacked[0], stacked[1]]).reshape(2, MB, SEQS, LEN, D).astype(jnp.bfloat16)
    input_grads = jnp.stack([stacked[2], stacked[3]]).reshape(2, MB, SEQS, LEN, D).astype(jnp.bfloat16)
    return (section_outputs, input_grads, sums[0], sums[1])
```

```python
from functools import partial

import jax
import jax.numpy as jnp
from jax import lax
from jax.experimental import pallas as pl
from jax.experimental.pallas import tpu as pltpu
from jax.sharding import PartitionSpec as P

D = 768
HEADS = 12
HEAD_DIM = 64
FF = 3072
RANK = 1024
LEN = 512
CUT = 256

epsilon = 1e-05
bf16 = jnp.bfloat16
f32 = jnp.float32

HBM = pltpu.HBM
VMEM = pltpu.VMEM
SMEM = pltpu.SMEM


def dg(left, right, left_dim, right_dim):
    return lax.dot_general(
        left, right, (((left_dim,), (right_dim,)), ((), ())), preferred_element_type=f32
    )


def head_rows(head):
    return slice(HEAD_DIM * head, HEAD_DIM * (head + 1))


def cuts(total, size):
    return [slice(start, start + size) for start in range(0, total, size)]


def fill_bias(bias, lengths, padding, seq):
    bounds = []
    total = 0
    for j in range(lengths.shape[2] - 1):
        total = total + lengths[seq, 0, j]
        bounds.append(total)
    key_pos = lax.broadcasted_iota(jnp.int32, (LEN, 1), 0)
    query_pos = lax.broadcasted_iota(jnp.int32, (1, LEN), 1)
    key_doc = sum((key_pos >= b).astype(jnp.int32) for b in bounds)
    query_doc = sum((query_pos >= b).astype(jnp.int32) for b in bounds)
    key_doc = jnp.where(key_pos < LEN - padding[seq, 0], key_doc, -1)
    seen = (key_doc == query_doc) | (key_pos == query_pos)
    bias[...] = jnp.where(seen, 0.0, -1e30)


def norm_rows(values):
    average = jnp.mean(values, axis=-1, keepdims=True)
    centered = values - average
    variance = jnp.mean(centered * centered, axis=-1, keepdims=True)
    inv_std = lax.rsqrt(variance + epsilon)
    return centered * inv_std, inv_std


def norm_back(normal, inv_std, scaled):
    return inv_std * (
        scaled
        - jnp.mean(scaled, axis=-1, keepdims=True)
        - normal * jnp.mean(scaled * normal, axis=-1, keepdims=True)
    )


def rank_forward(h, lower, upper, ranks, reduced, rank_q, rank_v, vera_q, vera_v):
    for c in cuts(RANK, CUT):
        part = dg(h[...], lower[c, :], 1, 1)
        reduced[:, c] = part.astype(bf16)
        rank_q[:, c] = (ranks[0:1, c] * part).astype(bf16)
        rank_v[:, c] = (ranks[1:2, c] * part).astype(bf16)
    for c in cuts(D, CUT):
        vera_q[c, :] = dg(upper[c, :], rank_q[...], 1, 1).astype(vera_q.dtype)
        vera_v[c, :] = dg(upper[c, :], rank_v[...], 1, 1).astype(vera_v.dtype)


def project(h, w_q, w_k, w_v, columns, vera_q, vera_v, queries, keys, values):
    for c in cuts(D, CUT):
        part = dg(w_q[:, c], h[...], 0, 1)
        part = part + columns[c, 0:1] + columns[c, 8:9] * vera_q[c, :].astype(f32)
        queries[c, :] = part.astype(bf16) * jnp.asarray(HEAD_DIM**-0.5, bf16)
    for c in cuts(D, CUT):
        keys[c, :] = dg(w_k[:, c], h[...], 0, 1).astype(bf16)
    for c in cuts(D, CUT):
        part = dg(w_v[:, c], h[...], 0, 1)
        part = part + columns[c, 1:2] + columns[c, 9:10] * vera_v[c, :].astype(f32)
        values[c, :] = part.astype(bf16)


def attend(queries, keys, values, bias, score, expon, inverse, context):
    for t in range(HEADS + 2):
        if t < HEADS:
            r = head_rows(t)
            score[t % 2] = dg(keys[r, :], queries[r, :], 0, 0)
        if 0 <= t - 2:
            r = head_rows(t - 2)
            part = dg(values[r, :], expon[t - 2], 1, 0) * inverse[t - 2 : t - 1, :]
            context[r, :] = part.astype(bf16)
        if 0 <= t - 1 < HEADS:
            masked = score[(t - 1) % 2] + bias[...]
            e = jnp.exp(masked - jnp.max(masked, axis=0, keepdims=True))
            inverse[t - 1 : t, :] = 1.0 / jnp.sum(e, axis=0, keepdims=True)
            expon[t - 1] = e.astype(bf16)


def first_norm(h, context, w_out, vectors, normed, normed_low, normal, inv_std):
    for c in cuts(LEN, CUT):
        total = dg(context[:, c], w_out[...], 0, 0) + h[c, :].astype(f32) + vectors[2:3, :]
        xhat, s = norm_rows(total)
        normal[c, :] = xhat.astype(bf16)
        inv_std[c, :] = s
        out = xhat * vectors[3:4, :] + vectors[4:5, :]
        normed[c, :] = out
        normed_low[c, :] = out.astype(bf16)


def widen(normed_low, w_up, up_bias, active, slope):
    for c in cuts(FF, 2 * CUT):
        x = dg(normed_low[...], w_up[:, c], 1, 0) + up_bias[:, c]
        share = 0.5 + 0.5 * lax.erf(x * 0.7071067811865476)
        active[:, c] = (x * share).astype(bf16)
        bell = jnp.exp(x * x * -0.5) * 0.3989422804014327
        slope[:, c] = (share + x * bell).astype(bf16)


def narrow(active, w_down, vectors, normed, result, normal, inv_std):
    for c in cuts(LEN, CUT):
        total = dg(active[c, :], w_down[...], 1, 0) + normed[c, :] + vectors[5:6, :]
        xhat, s = norm_rows(total)
        normal[c, :] = xhat.astype(bf16)
        inv_std[c, :] = s
        result[c, :] = (xhat * vectors[6:7, :] + vectors[7:8, :]).astype(bf16)


def second_back(g, vectors, normal, inv_std, wide, low):
    for c in cuts(LEN, CUT):
        scaled = g[c, :].astype(f32) * vectors[6:7, :]
        out = norm_back(normal[c, :].astype(f32), inv_std[c, :], scaled)
        wide[c, :] = out
        low[c, :] = out.astype(bf16)


def feed_back(low, w_down, slope, grad_before):
    for c in cuts(FF, 2 * CUT):
        part = dg(low[...], w_down[c, :], 1, 1)
        grad_before[:, c] = (part * slope[:, c].astype(f32)).astype(bf16)


def first_back(grad_before, w_up, vectors, normal, inv_std, wide, low):
    for c in cuts(LEN, CUT):
        grad = dg(grad_before[c, :], w_up[...], 1, 1) + wide[c, :]
        out = norm_back(normal[c, :].astype(f32), inv_std[c, :], grad * vectors[3:4, :])
        wide[c, :] = out
        low[c, :] = out.astype(bf16)


def context_back(low, w_out, inverse, context, grad_context, delta):
    for c in cuts(D, CUT):
        part = dg(w_out[c, :], low[...], 1, 1)
        for n in range(CUT // HEAD_DIM):
            head = c.start // HEAD_DIM + n
            r = head_rows(head)
            own = (part[head_rows(n), :] * inverse[head : head + 1, :]).astype(bf16)
            grad_context[r, :] = own
            delta[head : head + 1, :] = jnp.sum(
                own.astype(f32) * context[r, :].astype(f32), axis=0, keepdims=True
            )


def attend_back(
    queries, keys, values, expon, grad_context, delta, score, grad_score, grad_q, grad_k, grad_v
):
    for t in range(HEADS + 2):
        if t < HEADS:
            r = head_rows(t)
            score[t % 2] = dg(values[r, :], grad_context[r, :], 0, 0)
        if 0 <= t - 2:
            r = head_rows(t - 2)
            own = grad_score.at[t % 2]
            grad_q[r, :] = (dg(keys[r, :], own[...], 1, 0) * HEAD_DIM**-0.5).astype(bf16)
            grad_v[r, :] = dg(grad_context[r, :], expon[t - 2], 1, 1).astype(bf16)
            grad_k[r, :] = dg(queries[r, :], own[...], 1, 1).astype(bf16)
        if 0 <= t - 1 < HEADS:
            part = score[(t - 1) % 2] - delta[t - 1 : t, :]
            grad_score[(t - 1) % 2] = (expon[t - 1].astype(f32) * part).astype(bf16)


def rank_back(
    grad_q, grad_v, columns, upper, ranks, reduced, vera_q, vera_v, grad_reduced, width_sum, rank_sum
):
    sums = []
    for grad, vera, column in ((grad_q, vera_q, 8), (grad_v, vera_v, 9)):
        wide = grad[...].astype(f32)
        sums.append(jnp.sum(vera[...].astype(f32) * wide, axis=1, keepdims=True))
        vera[...] = (columns[:, column : column + 1] * wide).astype(bf16)
    width_sum[...] = jnp.concatenate(
        [jnp.transpose(jnp.broadcast_to(s, (D, 128)))[0:1, :] for s in sums], axis=0
    )
    for c in cuts(RANK, CUT):
        part_q = dg(vera_q[...], upper[:, c], 0, 0)
        part_v = dg(vera_v[...], upper[:, c], 0, 0)
        own = reduced[:, c].astype(f32)
        rank_sum[0:1, c] = jnp.sum(own * part_q, axis=0, keepdims=True)
        rank_sum[1:2, c] = jnp.sum(own * part_v, axis=0, keepdims=True)
        grad_reduced[:, c] = (ranks[0:1, c] * part_q + ranks[1:2, c] * part_v).astype(bf16)


def input_back(wide, grad_q, grad_k, grad_v, grad_reduced, w_q, w_k, w_v, lower, result):
    for c in cuts(LEN, CUT):
        total = wide[c, :] + dg(grad_q[:, c], w_q[...], 0, 1)
        total = total + dg(grad_k[:, c], w_k[...], 0, 1)
        total = total + dg(grad_v[:, c], w_v[...], 0, 1)
        total = total + dg(grad_reduced[c, :], lower[...], 1, 0)
        result[c, :] = total.astype(bf16)


class Loads:
    def __init__(self, sems):
        self.sems = sems
        self.count = 0

    def start(self, source, target):
        copy = pltpu.make_async_copy(source, target, self.sems.at[self.count])
        self.count += 1
        copy.start()
        return copy

    def pick(self, condition, source, other, target):
        sem = self.sems.at[self.count]
        self.count += 1

        @pl.when(condition)
        def _():
            pltpu.make_async_copy(source, target, sem).start()

        @pl.when(jnp.logical_not(condition))
        def _():
            pltpu.make_async_copy(other, target, sem).start()

        return pltpu.make_async_copy(source, target, sem)


def choose(condition, own, other):
    return jnp.where(condition, own, other)


def make_columns(vectors, widths):
    rows = jnp.concatenate([vectors, widths, jnp.zeros((6, D), f32)], axis=0)
    return jnp.transpose(rows)


def rank_kernel(
    sec, inputs, lower, upper, ranks_own, ranks_got,
    reduced, vera_q, vera_v,
    h, low_v, up_v, ranks, rank_q, rank_v, sems,
):
    seq = sec[0]
    loads = Loads(sems)
    waits = [
        loads.start(inputs.at[seq, 0], h),
        loads.start(lower, low_v),
        loads.start(upper, up_v),
    ]
    ranks[...] = choose(seq == 0, ranks_own[0], ranks_got[0])
    for w in waits:
        w.wait()
    rank_forward(h, low_v, up_v, ranks, reduced, rank_q, rank_v, vera_q, vera_v)


def attend_kernel(
    sec, lengths, padding, inputs, qkv_own, qkv_got, vec_own, vec_got, width_own, width_got,
    vera_q, vera_v,
    queries, keys, values, expon, inverse, context,
    h, qkv, bias, columns, score, sems,
):
    seq = sec[0]
    loads = Loads(sems)
    mine = seq == 0
    wait_h = loads.start(inputs.at[seq, 0], h)
    waits = [loads.pick(mine, qkv_own.at[0, n], qkv_got.at[0, n], qkv.at[n]) for n in range(3)]
    columns[...] = make_columns(
        choose(mine, vec_own[0], vec_got[0]), choose(mine, width_own[0], width_got[0])
    )
    fill_bias(bias, lengths, padding, seq)
    wait_h.wait()
    for w in waits:
        w.wait()
    project(h, qkv.at[0], qkv.at[1], qkv.at[2], columns, vera_q, vera_v, queries, keys, values)
    attend(queries, keys, values, bias, score, expon, inverse, context)


def widen_kernel(
    sec, inputs, context, out_own, out_got, up_own, up_got, vec_own, vec_got, bias_own, bias_got,
    normed, normal, inv_std, active, slope,
    h, w_out, w_up, normed_low, sems,
):
    seq = sec[0]
    loads = Loads(sems)
    mine = seq == 0
    wait_h = loads.start(inputs.at[seq, 0], h)
    wait_out = loads.pick(mine, out_own.at[0], out_got.at[0], w_out)
    wait_up = loads.pick(mine, up_own.at[0], up_got.at[0], w_up)
    vectors = choose(mine, vec_own[0], vec_got[0])
    up_bias = choose(mine, bias_own[...], bias_got[...])
    wait_h.wait()
    wait_out.wait()
    first_norm(h, context, w_out, vectors, normed, normed_low, normal, inv_std)
    wait_up.wait()
    widen(normed_low, w_up, up_bias, active, slope)


def narrow_kernel(
    sec, active, normed, down_own, down_got, vec_own, vec_got,
    result, normal, inv_std,
    w_down, sems,
):
    mine = sec[0] == 0
    wait = Loads(sems).pick(mine, down_own.at[0], down_got.at[0], w_down)
    vectors = choose(mine, vec_own[0], vec_got[0])
    wait.wait()
    narrow(active, w_down, vectors, normed, result, normal, inv_std)


def layer_kernel(
    sec, lengths, padding, h, cotangent, lower, upper,
    qkv_own, qkv_got, out_own, out_got, up_own, up_got, down_own, down_got,
    vec_own, vec_got, bias_own, bias_got, ranks_own, ranks_got, width_own, width_got,
    result, grad_rows, rank_sum, width_sum,
    g, low_v, up_v, qkv, w_out, w_up, w_down, ranks, columns, reduced, rank_q, rank_v,
    vera_q, vera_v, queries, keys, values, bias, score, expon, inverse, context,
    wide, low, normal_1, inv_std_1, normal_2, inv_std_2, active, slope,
    grad_context, delta, grad_score, grad_q, grad_k, grad_v, sems,
):
    seq = sec[0]
    mine = seq == 1
    loads = Loads(sems)
    wait_lower = loads.start(lower, low_v)
    wait_upper = loads.start(upper, up_v)
    waits = [loads.pick(mine, qkv_own.at[0, n], qkv_got.at[0, n], qkv.at[n]) for n in range(3)]
    wait_out = loads.pick(mine, out_own.at[0], out_got.at[0], w_out)
    wait_up = loads.pick(mine, up_own.at[0], up_got.at[0], w_up)
    wait_down = loads.pick(mine, down_own.at[0], down_got.at[0], w_down)
    wait_g = loads.start(cotangent.at[seq, 0], g)
    vectors = choose(mine, vec_own[0], vec_got[0])
    up_bias = choose(mine, bias_own[...], bias_got[...])
    columns[...] = make_columns(vectors, choose(mine, width_own[0], width_got[0]))
    ranks[...] = choose(mine, ranks_own[0], ranks_got[0])
    fill_bias(bias, lengths, padding, seq)
    wait_lower.wait()
    wait_upper.wait()
    rank_forward(h, low_v, up_v, ranks, reduced, rank_q, rank_v, vera_q, vera_v)
    for w in waits:
        w.wait()
    w_q, w_k, w_v = qkv.at[0], qkv.at[1], qkv.at[2]
    project(h, w_q, w_k, w_v, columns, vera_q, vera_v, queries, keys, values)
    attend(queries, keys, values, bias, score, expon, inverse, context)
    wait_out.wait()
    first_norm(h, context, w_out, vectors, wide, low, normal_1, inv_std_1)
    wait_up.wait()
    widen(low, w_up, up_bias, active, slope)
    wait_down.wait()
    narrow(active, w_down, vectors, wide, result, normal_2, inv_std_2)
    wait_g.wait()
    second_back(g, vectors, normal_2, inv_std_2, wide, low)
    feed_back(low, w_down, slope, active)
    first_back(active, w_up, vectors, normal_1, inv_std_1, wide, low)
    context_back(low, w_out, inverse, context, grad_context, delta)
    attend_back(
        queries, keys, values, expon, grad_context, delta, score, grad_score, grad_q, grad_k, grad_v
    )
    rank_back(
        grad_q, grad_v, columns, up_v, ranks, reduced, vera_q, vera_v, rank_q, width_sum, rank_sum
    )
    input_back(wide, grad_q, grad_k, grad_v, rank_q, w_q, w_k, w_v, low_v, grad_rows)


def back_kernel(
    sec, g, upper, out_own, out_got, up_own, up_got, down_own, down_got,
    vec_own, vec_got, ranks_own, ranks_got, width_own, width_got,
    reduced, vera_q, vera_v, queries, keys, values, expon, inverse, context,
    normal_1, inv_std_1, slope, normal_2, inv_std_2,
    wide, grad_q, grad_k, grad_v, grad_reduced, rank_sum, width_sum,
    up_v, w_out, w_up, w_down, ranks, columns, low, grad_before, grad_context, delta, score, grad_score,
    q_s, k_s, v_s, e_s, red_s, vq_s, vv_s, sl_s, n1_s, ctx_s, sems,
):
    mine = sec[0] == 0
    loads = Loads(sems)
    wait_down = loads.pick(mine, down_own.at[0], down_got.at[0], w_down)
    wait_slope = loads.start(slope, sl_s)
    wait_up = loads.pick(mine, up_own.at[0], up_got.at[0], w_up)
    wait_n1 = loads.start(normal_1, n1_s)
    wait_out = loads.pick(mine, out_own.at[0], out_got.at[0], w_out)
    wait_ctx = loads.start(context, ctx_s)
    waits = [
        loads.start(values, v_s),
        loads.start(expon, e_s),
        loads.start(keys, k_s),
        loads.start(queries, q_s),
    ]
    late = [
        loads.start(upper, up_v),
        loads.start(reduced, red_s),
        loads.start(vera_q, vq_s),
        loads.start(vera_v, vv_s),
    ]
    vectors = choose(mine, vec_own[0], vec_got[0])
    columns[...] = make_columns(vectors, choose(mine, width_own[0], width_got[0]))
    ranks[...] = choose(mine, ranks_own[0], ranks_got[0])
    second_back(g, vectors, normal_2, inv_std_2, wide, low)
    wait_down.wait()
    wait_slope.wait()
    feed_back(low, w_down, sl_s, grad_before)
    wait_up.wait()
    wait_n1.wait()
    first_back(grad_before, w_up, vectors, n1_s, inv_std_1, wide, low)
    wait_out.wait()
    wait_ctx.wait()
    context_back(low, w_out, inverse, ctx_s, grad_context, delta)
    for w in waits:
        w.wait()
    attend_back(
        q_s, k_s, v_s, e_s, grad_context, delta, score, grad_score, grad_q, grad_k, grad_v
    )
    for w in late:
        w.wait()
    rank_back(
        grad_q, grad_v, columns, up_v, ranks, red_s, vq_s, vv_s, grad_reduced, width_sum, rank_sum
    )


def input_kernel(
    sec, wide, grad_q, grad_k, grad_v, grad_reduced, qkv_own, qkv_got, lower,
    grad_rows,
    qkv, low_v, sems,
):
    mine = sec[0] == 0
    loads = Loads(sems)
    waits = [loads.pick(mine, qkv_own.at[0, n], qkv_got.at[0, n], qkv.at[n]) for n in range(3)]
    waits.append(loads.start(lower, low_v))
    for w in waits:
        w.wait()
    input_back(
        wide, grad_q, grad_k, grad_v, grad_reduced, qkv.at[0], qkv.at[1], qkv.at[2], low_v, grad_rows
    )


def shape(*dims, dtype=bf16):
    return jax.ShapeDtypeStruct(dims, dtype)


def call(kernel, name, operands, outs, scratch, copies, gmacs, megabytes=60):
    result = pl.pallas_call(
        kernel,
        name=name,
        in_specs=[pl.BlockSpec(memory_space=space) for space, _ in operands],
        out_specs=[pl.BlockSpec(memory_space=VMEM) for _ in outs],
        out_shape=outs,
        scratch_shapes=[VMEM(s.shape, s.dtype) for s in scratch]
        + [pltpu.SemaphoreType.DMA((copies,))],
        compiler_params=pltpu.CompilerParams(vmem_limit_bytes=megabytes * 2**20),
        cost_estimate=pl.CostEstimate(
            flops=int(2e9 * gmacs), bytes_accessed=2**20, transcendentals=0
        ),
    )(*[array for _, array in operands])
    return result


ROWS = shape(LEN, D)
WIDE = shape(LEN, D, dtype=f32)
TALL = shape(D, LEN)
SPREAD = shape(LEN, FF)
RANKED = shape(LEN, RANK)
LOWER = shape(RANK, D)
UPPER = shape(D, RANK)
QKV = shape(3, D, D)
OUT = shape(D, D)
UP = shape(D, FF)
DOWN = shape(FF, D)
EXPON = shape(HEADS, LEN, LEN)
PER_HEAD = shape(16, LEN, dtype=f32)
SCORE = shape(2, LEN, LEN, dtype=f32)
SCORE_LOW = shape(2, LEN, LEN)
BIAS = shape(LEN, LEN, dtype=f32)
INV_STD = shape(LEN, 1, dtype=f32)
COLUMNS = shape(D, 16, dtype=f32)
RANKS = shape(2, RANK, dtype=f32)
WIDTHS = shape(2, D, dtype=f32)


def spread_sum(block, axis):
    size = lax.axis_size(axis)
    if size & (size - 1):
        return lax.psum(block, axis)
    step = 1
    while step < size:
        block = block + lax.ppermute(block, axis, [(i, i ^ step) for i in range(size)])
        step *= 2
    return block


def body(
    inputs, cotangent, pair_lengths, padding, qkv_weights, out_weights, up_weights, down_weights,
    layer_vectors, up_biases, shared_in, shared_out, scale_rank, scale_width,
):
    section = lax.axis_index("section").astype(jnp.int32)
    sec = section.reshape(1)

    def swap(block):
        return lax.ppermute(block, "section", [(0, 1), (1, 0)])

    def both(space, own, got):
        return [(space, own), (space, got)]

    ranks = both(VMEM, scale_rank, swap(scale_rank))
    widths = both(VMEM, scale_width, swap(scale_width))
    vectors = both(VMEM, layer_vectors, swap(layer_vectors))
    biases = both(VMEM, up_biases, swap(up_biases))
    qkv = both(HBM, qkv_weights, swap(qkv_weights))
    w_out = both(HBM, out_weights, swap(out_weights))
    w_up = both(HBM, up_weights, swap(up_weights))
    w_down = both(HBM, down_weights, swap(down_weights))
    lower = (HBM, shared_in)
    upper = (HBM, shared_out)
    sec = (SMEM, sec)
    lengths = (SMEM, pair_lengths)
    pads = (SMEM, padding)
    rows = (HBM, inputs)

    reduced, vera_q, vera_v = call(
        rank_kernel, "ranks", [sec, rows, lower, upper] + ranks,
        [RANKED, TALL, TALL],
        [ROWS, LOWER, UPPER, RANKS, RANKED, RANKED], 3, 1.2,
    )
    queries, keys, values, expon, inverse, context = call(
        attend_kernel, "attention",
        [sec, lengths, pads, rows] + qkv + vectors + widths + [(VMEM, vera_q), (VMEM, vera_v)],
        [TALL, TALL, TALL, EXPON, PER_HEAD, TALL],
        [ROWS, QKV, BIAS, COLUMNS, SCORE], 4, 2.5,
    )
    normed, normal_1, inv_std_1, active, slope = call(
        widen_kernel, "widen",
        [sec, rows, (VMEM, context)] + w_out + w_up + vectors + biases,
        [WIDE, ROWS, INV_STD, SPREAD, SPREAD],
        [ROWS, OUT, UP, ROWS], 3, 1.5,
    )
    first, normal_2, inv_std_2 = call(
        narrow_kernel, "narrow",
        [sec, (VMEM, active), (VMEM, normed)] + w_down + vectors,
        [ROWS, ROWS, INV_STD],
        [DOWN], 1, 1.2,
    )
    second, upstream, rank_1, width_1 = call(
        layer_kernel, "second_layer",
        [sec, lengths, pads, (VMEM, first), (HBM, cotangent), lower, upper]
        + qkv + w_out + w_up + w_down + vectors + biases + ranks + widths,
        [ROWS, ROWS, RANKS, WIDTHS],
        [ROWS, LOWER, UPPER, QKV, OUT, UP, DOWN, RANKS, COLUMNS, RANKED, RANKED, RANKED,
         TALL, TALL, TALL, TALL, TALL, BIAS, SCORE, EXPON, PER_HEAD, TALL,
         WIDE, ROWS, ROWS, INV_STD, ROWS, INV_STD, SPREAD, SPREAD,
         TALL, PER_HEAD, SCORE_LOW, TALL, TALL, TALL],
        9, 14.0,
    )
    wide, grad_q, grad_k, grad_v, grad_reduced, rank_0, width_0 = call(
        back_kernel, "first_back",
        [sec, (VMEM, upstream), upper] + w_out + w_up + w_down + vectors + ranks + widths
        + [(HBM, a) for a in (reduced, vera_q, vera_v, queries, keys, values, expon)]
        + [(VMEM, inverse), (HBM, context), (HBM, normal_1), (VMEM, inv_std_1), (HBM, slope)]
        + [(VMEM, normal_2), (VMEM, inv_std_2)],
        [WIDE, TALL, TALL, TALL, RANKED, RANKS, WIDTHS],
        [UPPER, OUT, UP, DOWN, RANKS, COLUMNS, ROWS, SPREAD, TALL, PER_HEAD, SCORE, SCORE_LOW,
         TALL, TALL, TALL, EXPON, RANKED, TALL, TALL, SPREAD, ROWS, TALL],
        14, 6.0,
    )
    leading = section == 0

    def assemble(own_first, own_second):
        got = swap(jnp.where(leading, own_second, own_first))
        kept = jnp.where(leading, own_first, own_second)
        parts = [jnp.where(leading, kept, got), jnp.where(leading, got, kept)]
        return jnp.stack(parts)[None, :, None]

    section_outputs = assemble(first, second)

    def packed(rank, width):
        return jnp.concatenate([rank.reshape(-1), width.reshape(-1)]).reshape(-1, 128)

    sums_0, sums_1 = packed(rank_0, width_0), packed(rank_1, width_1)
    sums = jnp.where(leading, sums_0, sums_1) + swap(jnp.where(leading, sums_1, sums_0))
    sums = spread_sum(sums, "dp").reshape(-1)
    (grad_rows,) = call(
        input_kernel, "first_inputs",
        [sec] + [(VMEM, a) for a in (wide, grad_q, grad_k, grad_v, grad_reduced)] + qkv + [lower],
        [ROWS],
        [QKV, LOWER], 4, 1.3,
    )
    input_grads = assemble(grad_rows, upstream)
    total_rank = sums[: 2 * RANK].reshape(1, 2, RANK)
    total_width = sums[2 * RANK :].reshape(1, 2, D)
    return section_outputs, input_grads, total_rank, total_width


def solution(mesh):
    in_specs = (
        P(None, "dp", None, None),
        P(None, "dp", None, None),
        P(None, "dp", None),
        P(None, "dp"),
        P("section", None, None, None),
        P("section", None, None),
        P("section", None, None),
        P("section", None, None),
        P("section", None, None),
        P("section", None),
        P(),
        P(),
        P("section", None, None),
        P("section", None, None),
    )
    out_specs = (
        P("section", None, "dp", None, None),
        P("section", None, "dp", None, None),
        P("section", None, None),
        P("section", None, None),
    )
    return jax.shard_map(body, mesh=mesh, in_specs=in_specs, out_specs=out_specs, check_vma=False)
```

```python
import jax
import jax.numpy as jnp
from jax import lax
from jax.experimental import pallas as pl
from jax.experimental.pallas import tpu as pltpu
from jax.sharding import PartitionSpec as P

D = 768
HEADS = 12
HEAD_DIM = 64
FF = 3072
RANK = 1024
LEN = 512
CUT = 256

epsilon = 1e-05
bf16 = jnp.bfloat16
f32 = jnp.float32

HBM = pltpu.HBM
VMEM = pltpu.VMEM
SMEM = pltpu.SMEM


def dg(left, right, left_dim, right_dim):
    return lax.dot_general(
        left, right, (((left_dim,), (right_dim,)), ((), ())), preferred_element_type=f32
    )


def head_rows(head):
    return slice(HEAD_DIM * head, HEAD_DIM * (head + 1))


def cuts(total, size):
    return [slice(start, start + size) for start in range(0, total, size)]


def fill_bias(bias, lengths, padding, seq):
    bounds = []
    total = 0
    for j in range(lengths.shape[2] - 1):
        total = total + lengths[seq, 0, j]
        bounds.append(total)
    key_pos = lax.broadcasted_iota(jnp.int32, (LEN, 1), 0)
    query_pos = lax.broadcasted_iota(jnp.int32, (1, LEN), 1)
    key_doc = sum((key_pos >= b).astype(jnp.int32) for b in bounds)
    query_doc = sum((query_pos >= b).astype(jnp.int32) for b in bounds)
    key_doc = jnp.where(key_pos < LEN - padding[seq], key_doc, -1)
    seen = (key_doc == query_doc) | (key_pos == query_pos)
    bias[...] = jnp.where(seen, 0.0, -1e30)


def norm_rows(values):
    average = jnp.mean(values, axis=-1, keepdims=True)
    centered = values - average
    variance = jnp.mean(centered * centered, axis=-1, keepdims=True)
    inv_std = lax.rsqrt(variance + epsilon)
    return centered * inv_std, inv_std


def norm_back(normal, inv_std, scaled):
    return inv_std * (
        scaled
        - jnp.mean(scaled, axis=-1, keepdims=True)
        - normal * jnp.mean(scaled * normal, axis=-1, keepdims=True)
    )


def rank_lower(h, lower, ranks, reduced, rank_q, rank_v):
    for c in cuts(RANK, CUT):
        part = dg(h[...], lower[c, :], 1, 1)
        reduced[:, c] = part.astype(bf16)
        rank_q[:, c] = (ranks[0:1, c] * part).astype(bf16)
        rank_v[:, c] = (ranks[1:2, c] * part).astype(bf16)


def rank_upper(upper, rank, vera):
    for c in cuts(D, CUT):
        vera[c, :] = dg(upper[c, :], rank[...], 1, 1).astype(bf16)


def project_queries(h, weights, columns, vera, queries):
    for c in cuts(D, CUT):
        part = dg(weights[:, c], h[...], 0, 1)
        part = part + columns[c, 0:1] + columns[c, 8:9] * vera[c, :].astype(f32)
        queries[c, :] = part.astype(bf16) * jnp.asarray(HEAD_DIM**-0.5, bf16)


def project_keys(h, weights, keys):
    for c in cuts(D, CUT):
        keys[c, :] = dg(weights[:, c], h[...], 0, 1).astype(bf16)


def project_values(h, weights, columns, vera, values):
    for c in cuts(D, CUT):
        part = dg(weights[:, c], h[...], 0, 1)
        part = part + columns[c, 1:2] + columns[c, 9:10] * vera[c, :].astype(f32)
        values[c, :] = part.astype(bf16)


def attend(queries, keys, values, bias, score, expon, inverse, context, done=None):
    for t in range(HEADS + 2):
        if t < HEADS:
            r = head_rows(t)
            score[t % 2] = dg(keys[r, :], queries[r, :], 0, 0)
        if 0 <= t - 2:
            r = head_rows(t - 2)
            part = dg(values[r, :], expon(t - 2)[...], 1, 0) * inverse[t - 2 : t - 1, :]
            context[r, :] = part.astype(bf16)
        if 0 <= t - 1 < HEADS:
            masked = score[(t - 1) % 2] + bias[...]
            e = jnp.exp(masked - jnp.max(masked, axis=0, keepdims=True))
            inverse[t - 1 : t, :] = 1.0 / jnp.sum(e, axis=0, keepdims=True)
            expon(t - 1)[...] = e.astype(bf16)
            if done is not None:
                done(t - 1)


def first_norm(h, context, w_out, vectors, normed, normed_low, normal, inv_std):
    for c in cuts(LEN, CUT):
        total = dg(context[:, c], w_out[...], 0, 0) + h[c, :].astype(f32) + vectors[2:3, :]
        xhat, s = norm_rows(total)
        normal[c, :] = xhat.astype(bf16)
        inv_std[c, :] = jnp.broadcast_to(s, (CUT, 128))
        out = xhat * vectors[3:4, :] + vectors[4:5, :]
        normed[c, :] = out
        normed_low[c, :] = out.astype(bf16)


def widen(normed_low, w_up, up_bias, active, slope, part):
    for start in range(part.start, part.stop, CUT):
        c = slice(start, start + CUT)
        x = dg(normed_low[...], w_up[:, c], 1, 0) + up_bias[:, c]
        share = 0.5 + 0.5 * lax.erf(x * 0.7071067811865476)
        active[:, c] = (x * share).astype(bf16)
        bell = jnp.exp(x * x * -0.5) * 0.3989422804014327
        slope[:, c] = (share + x * bell).astype(bf16)


def narrow(active, w_down, vectors, normed, result, normal, inv_std):
    for c in cuts(LEN, CUT):
        total = dg(active[c, :], w_down[...], 1, 0) + normed[c, :] + vectors[5:6, :]
        close_layer(total, c, vectors, result, normal, inv_std)


def close_layer(total, c, vectors, result, normal, inv_std):
    xhat, s = norm_rows(total)
    normal[c, :] = xhat.astype(bf16)
    inv_std[c, :] = jnp.broadcast_to(s, (CUT, 128))
    result[c, :] = (xhat * vectors[6:7, :] + vectors[7:8, :]).astype(bf16)


def second_back(g, vectors, normal, inv_std, wide, low):
    for c in cuts(LEN, CUT):
        scaled = g[c, :].astype(f32) * vectors[6:7, :]
        out = norm_back(normal[c, :].astype(f32), inv_std[c, 0:1], scaled)
        wide[c, :] = out
        low[c, :] = out.astype(bf16)


def feed_back(low, w_down, slope, grad_before):
    for c in cuts(FF, 2 * CUT):
        part = dg(low[...], w_down[c, :], 1, 1)
        grad_before[:, c] = (part * slope[:, c].astype(f32)).astype(bf16)


def first_back(grad_before, w_up, vectors, normal, inv_std, wide, low):
    for c in cuts(LEN, CUT):
        grad = dg(grad_before[c, :], w_up[...], 1, 1) + wide[c, :]
        out = norm_back(normal[c, :].astype(f32), inv_std[c, 0:1], grad * vectors[3:4, :])
        wide[c, :] = out
        low[c, :] = out.astype(bf16)


def context_back(low, w_out, inverse, context, grad_context, delta):
    for c in cuts(D, CUT):
        part = dg(w_out[c, :], low[...], 1, 1)
        for n in range(CUT // HEAD_DIM):
            head = c.start // HEAD_DIM + n
            r = head_rows(head)
            own = (part[head_rows(n), :] * inverse[head : head + 1, :]).astype(bf16)
            grad_context[r, :] = own
            delta[head : head + 1, :] = jnp.sum(
                own.astype(f32) * context[r, :].astype(f32), axis=0, keepdims=True
            )


def attend_back(
    queries, keys, values, expon, grad_context, delta, score, grad_score, grad_q, grad_k, grad_v
):
    for t in range(HEADS + 2):
        if t < HEADS:
            r = head_rows(t)
            score[t % 2] = dg(values[r, :], grad_context[r, :], 0, 0)
        if 0 <= t - 2:
            r = head_rows(t - 2)
            own = grad_score.at[t % 2]
            grad_q[r, :] = (dg(keys[r, :], own[...], 1, 0) * HEAD_DIM**-0.5).astype(bf16)
            grad_v[r, :] = dg(grad_context[r, :], expon(t - 2)[...], 1, 1).astype(bf16)
            grad_k[r, :] = dg(queries[r, :], own[...], 1, 1).astype(bf16)
        if 0 <= t - 1 < HEADS:
            part = score[(t - 1) % 2] - delta[t - 1 : t, :]
            grad_score[(t - 1) % 2] = (expon(t - 1)[...].astype(f32) * part).astype(bf16)


def rank_back(
    grad_q, grad_v, columns, upper, ranks, reduced, vera_q, vera_v, grad_reduced, sums
):
    totals = []
    for grad, vera, column in ((grad_q, vera_q, 8), (grad_v, vera_v, 9)):
        wide = grad[...].astype(f32)
        totals.append(jnp.sum(vera[...].astype(f32) * wide, axis=1, keepdims=True))
        vera[...] = (columns[:, column : column + 1] * wide).astype(bf16)
    lane = lax.broadcasted_iota(jnp.int32, (D, 128), 1)
    turned = jnp.transpose(jnp.where(lane == 0, totals[0], totals[1]))
    sums[2:4, :D] = turned[0:2, :]
    sums[2:4, D:] = jnp.zeros((2, RANK - D), f32)
    for c in cuts(RANK, CUT):
        part_q = dg(vera_q[...], upper[:, c], 0, 0)
        part_v = dg(vera_v[...], upper[:, c], 0, 0)
        own = reduced[:, c].astype(f32)
        sums[0:1, c] = jnp.sum(own * part_q, axis=0, keepdims=True)
        sums[1:2, c] = jnp.sum(own * part_v, axis=0, keepdims=True)
        grad_reduced[:, c] = (ranks[0:1, c] * part_q + ranks[1:2, c] * part_v).astype(bf16)


def input_back(wide, grad_q, grad_k, grad_v, grad_reduced, w_q, w_k, w_v, lower, result):
    for c in cuts(LEN, CUT):
        total = wide[c, :] + dg(grad_q[:, c], w_q[...], 0, 1)
        total = total + dg(grad_k[:, c], w_k[...], 0, 1)
        total = total + dg(grad_v[:, c], w_v[...], 0, 1)
        total = total + dg(grad_reduced[c, :], lower[...], 1, 0)
        result[c, :] = total.astype(bf16)


class Copies:
    def __init__(self, sems):
        self.sems = sems
        self.count = 0

    def start(self, source, target):
        copy = pltpu.make_async_copy(source, target, self.sems.at[self.count])
        self.count += 1
        copy.start()
        return copy

    def pick(self, condition, one, other):
        sem = self.sems.at[self.count]
        self.count += 1

        @pl.when(condition)
        def _():
            pltpu.make_async_copy(*one, sem).start()

        @pl.when(jnp.logical_not(condition))
        def _():
            pltpu.make_async_copy(*other, sem).start()

        return pltpu.make_async_copy(*one, sem)

    def load(self, condition, pair, index, target):
        return self.pick(condition, (pair[0].at[index], target), (pair[1].at[index], target))


def wait(*copies):
    for copy in copies:
        copy.wait()


def choose(condition, pair):
    return jnp.where(condition, pair[0][0], pair[1][0])


def make_columns(vectors, widths):
    rows = jnp.concatenate([vectors, widths, jnp.zeros((6, D), f32)], axis=0)
    return jnp.transpose(rows)


def rank_kernel(
    sec, inputs, lower, upper, ranks_own, ranks_got,
    h, reduced, vera_q, vera_v,
    low_v, up_v, ranks, own, rank_q, rank_v, sems,
):
    seq = sec[0]
    copies = Copies(sems)
    first = [copies.start(inputs.at[seq, 0], h), copies.start(lower, low_v)]
    first.append(copies.start(ranks_own.at[0], own))
    second = copies.start(upper, up_v)
    wait(*first)
    ranks[...] = jnp.where(seq == 0, own[...], ranks_got[0])
    rank_lower(h, low_v, ranks, reduced, rank_q, rank_v)
    wait(second)
    rank_upper(up_v, rank_q, vera_q)
    rank_upper(up_v, rank_v, vera_v)


def attend_kernel(
    sec, lengths, padding, qkv_own, qkv_got, out_own, out_got, vec_own, vec_got, width_own, width_got,
    h, reduced, vera_q, vera_v,
    reduced_out, vera_q_out, vera_v_out, queries_out, keys_out, values_out, expon_out,
    context_out, normed_out, normed_low_out, normal_out, inv_std_out, inverse,
    qkv, w_out, queries, keys, values, expon, context, normed, normed_low, normal, inv_std,
    bias, columns, score, sems,
):
    seq = sec[0]
    copies = Copies(sems)
    mine = seq == 0
    vectors = choose(mine, (vec_own, vec_got))
    for n in (1, 0, 2):
        qkv[n] = jnp.where(mine, qkv_own[0, n], qkv_got[0, n])
    columns[...] = make_columns(vectors, choose(mine, (width_own, width_got)))
    fill_bias(bias, lengths, padding, seq)
    project_keys(h, qkv.at[1], keys)
    project_queries(h, qkv.at[0], columns, vera_q, queries)
    outs = [
        copies.start(reduced, reduced_out),
        copies.start(vera_q, vera_q_out),
        copies.start(vera_v, vera_v_out),
        copies.start(keys, keys_out),
        copies.start(queries, queries_out),
    ]
    project_values(h, qkv.at[2], columns, vera_v, values)
    outs.append(copies.start(values, values_out))

    def block(head):
        return expon.at[head]

    def done(head):
        outs.append(copies.start(expon.at[head], expon_out.at[head]))

    attend(queries, keys, values, bias, score, block, inverse, context, done)
    outs.append(copies.start(context, context_out))
    w_out[...] = jnp.where(mine, out_own[0], out_got[0])
    first_norm(h, context, w_out, vectors, normed, normed_low, normal, inv_std)
    outs += [
        copies.start(normed_low, normed_low_out),
        copies.start(normed, normed_out),
        copies.start(normal, normal_out),
        copies.start(inv_std, inv_std_out),
    ]
    wait(*outs)


def main_kernel(
    sec, lengths, padding, cotangent, lower, upper,
    qkv_own, qkv_got, out_own, out_got, up_own, up_got, down_own, down_got,
    vec_own, vec_got, bias_own, bias_got, ranks_own, ranks_got, width_own, width_got,
    reduced_0, vera_q_0, vera_v_0, queries_0, keys_0, values_0, expon_0,
    context_0, normed_0, normed_low_0, normal_0, inv_std_0, inverse_0,
    keep_sums, send_sums,
    section_outputs, input_grads, send_output, send_grad, slope_0,
    h, g, second, low_v, up_v, qkv, w_out, w_up, w_down, ranks, columns, reduced,
    vera_q, vera_v, queries, keys, values, bias, score, expon_v, inverse, context,
    low, normal_1, inv_std_1, normal_2, inv_std_2, first_2, first_2s,
    grad_context, delta, grad_score, grad_q, grad_k, grad_v, sums_0, sums_1, active, slope, wide, first_1, first_1s, sems,
):
    seq = sec[0]
    leading = seq == 0
    following = seq == 1
    copies = Copies(sems)
    w_qkv, w_o, w_u, w_d = (
        (qkv_own, qkv_got), (out_own, out_got), (up_own, up_got), (down_own, down_got),
    )
    vecs, biases = (vec_own, vec_got), (bias_own, bias_got)
    rank_pair, width_pair = (ranks_own, ranks_got), (width_own, width_got)
    w_q, w_k, w_v = qkv.at[0], qkv.at[1], qkv.at[2]
    rank_q, rank_v = active.at[:, 0:RANK], active.at[:, RANK : 2 * RANK]

    def expon(head):
        return expon_v.at[head]

    parts = cuts(FF, FF // 4)

    def load_up(c):
        return copies.pick(
            leading, (up_own.at[0, :, c], w_up.at[:, c]), (up_got.at[0, :, c], w_up.at[:, c])
        )

    def load_down(c):
        return copies.pick(
            leading, (down_own.at[0, c], w_down.at[c]), (down_got.at[0, c], w_down.at[c])
        )

    wait_low = copies.start(normed_low_0, low)
    wait_ups = [load_up(c) for c in parts[:2]]
    vectors = choose(leading, vecs)
    up_bias = jnp.where(leading, biases[0][...], biases[1][...])
    fill_bias(bias, lengths, padding, seq)
    wait(wait_low)
    outs = []
    for n, c in enumerate(parts):
        wait(wait_ups[n])
        if n == 0:
            wait_ups += [load_up(c) for c in parts[2:]]
        if n == 1:
            wait_down = [load_down(c) for c in parts]
            wait_normed = copies.start(normed_0, wide)
        if n == 2:
            wait_lower = copies.start(lower, low_v)
            wait_upper = copies.start(upper, up_v)
        widen(low, w_up, up_bias, active, slope, c)
        outs.append(copies.start(slope.at[:, c], slope_0.at[:, c]))
    wait(wait_normed, *wait_down)
    wait_up = copies.load(following, w_u, 0, w_up)
    wait_qkv = [copies.load(following, w_qkv, (0, n), qkv.at[n]) for n in range(3)]
    narrow(active, w_down, vectors, wide, h, first_2, first_2s)
    out_first = copies.pick(
        leading, (h, section_outputs.at[0, 0, 0]), (h, send_output)
    )

    vectors = choose(following, vecs)
    up_bias = jnp.where(following, biases[0][...], biases[1][...])
    columns[...] = make_columns(vectors, choose(following, width_pair))
    ranks[...] = choose(following, rank_pair)
    wait(wait_lower)
    rank_lower(h, low_v, ranks, reduced, rank_q, rank_v)
    wait(wait_upper)
    rank_upper(up_v, rank_q, vera_q)
    rank_upper(up_v, rank_v, vera_v)
    wait_out = copies.load(following, w_o, 0, w_out)
    wait_down = copies.load(following, w_d, 0, w_down)
    wait_g = copies.start(cotangent.at[seq, 0], g)
    wait_first = [copies.start(normal_0, first_1), copies.start(inv_std_0, first_1s)]
    wait(*wait_qkv)
    project_keys(h, w_k, keys)
    project_queries(h, w_q, columns, vera_q, queries)
    project_values(h, w_v, columns, vera_v, values)
    attend(queries, keys, values, bias, score, expon, inverse, context)
    wait(wait_out)
    first_norm(h, context, w_out, vectors, wide, low, normal_1, inv_std_1)
    wait(wait_up, *outs)
    for c in parts:
        widen(low, w_up, up_bias, active, slope, c)
    wait(wait_down)
    narrow(active, w_down, vectors, wide, second, normal_2, inv_std_2)
    out_second = copies.pick(
        following, (second, section_outputs.at[0, 1, 0]), (second, send_output)
    )

    wait(wait_g)
    second_back(g, vectors, normal_2, inv_std_2, wide, low)
    feed_back(low, w_down, slope, active)
    wait_down = copies.load(leading, w_d, 0, w_down)
    wait_slope = copies.start(slope_0, slope)
    first_back(active, w_up, vectors, normal_1, inv_std_1, wide, low)
    wait_up = copies.load(leading, w_u, 0, w_up)
    context_back(low, w_out, inverse, context, grad_context, delta)
    wait_out = copies.load(leading, w_o, 0, w_out)
    wait_context = copies.start(context_0, context)
    attend_back(
        queries, keys, values, expon, grad_context, delta, score, grad_score, grad_q, grad_k, grad_v
    )
    wait_attend = [
        copies.start(values_0, values),
        copies.start(expon_0, expon_v),
        copies.start(keys_0, keys),
        copies.start(queries_0, queries),
    ]
    rank_back(grad_q, grad_v, columns, up_v, ranks, reduced, vera_q, vera_v, rank_q, sums_1)
    wait_ranks = [
        copies.start(reduced_0, reduced),
        copies.start(vera_q_0, vera_q),
        copies.start(vera_v_0, vera_v),
    ]
    input_back(wide, grad_q, grad_k, grad_v, rank_q, w_q, w_k, w_v, low_v, g)
    wait_qkv = [copies.load(leading, w_qkv, (0, n), qkv.at[n]) for n in range(3)]
    out_upstream = copies.pick(
        following, (g, input_grads.at[0, 1, 0]), (g, send_grad)
    )

    vectors = choose(leading, vecs)
    columns[...] = make_columns(vectors, choose(leading, width_pair))
    ranks[...] = choose(leading, rank_pair)
    second_back(g, vectors, first_2, first_2s, wide, low)
    wait(wait_down, wait_slope)
    feed_back(low, w_down, slope, active)
    wait(wait_up, *wait_first)
    first_back(active, w_up, vectors, first_1, first_1s, wide, low)
    wait(wait_out, wait_context)
    context_back(low, w_out, inverse_0, context, grad_context, delta)
    wait(*wait_attend)
    attend_back(
        queries, keys, values, expon, grad_context, delta, score, grad_score, grad_q, grad_k, grad_v
    )
    wait(*wait_ranks)
    rank_back(grad_q, grad_v, columns, up_v, ranks, reduced, vera_q, vera_v, rank_q, sums_0)
    wait(*wait_qkv, out_second)
    input_back(wide, grad_q, grad_k, grad_v, rank_q, w_q, w_k, w_v, low_v, second)
    out_grad = copies.pick(
        leading, (second, input_grads.at[0, 0, 0]), (second, send_grad)
    )
    keep_sums[...] = jnp.where(leading, sums_0[...], sums_1[...])
    send_sums[...] = jnp.where(leading, sums_1[...], sums_0[...])
    wait(out_first, out_upstream, out_grad)


def finish_kernel(
    sec, got_output, got_grad, section_outputs, input_grads, outputs_out, grads_out, sems
):
    other = 1 - sec[0]
    copies = Copies(sems)
    wait(
        copies.start(got_output, outputs_out.at[0, other, 0]),
        copies.start(got_grad, grads_out.at[0, other, 0]),
    )


def shape(*dims, dtype=bf16):
    return jax.ShapeDtypeStruct(dims, dtype)


HELD = "held"


def call(kernel, name, operands, outs, scratch, copies, gmacs, megabytes, aliases={}):
    in_spaces = [VMEM if space is HELD else space for space, _ in operands]
    out_spaces = [VMEM if space is HELD else space for space, _ in outs]
    colour = {HELD: VMEM, HBM: HBM}
    arrays = [
        pltpu.with_memory_space_constraint(array, colour[space]) if space in colour else array
        for space, array in operands
    ]
    return pl.pallas_call(
        kernel,
        name=name,
        in_specs=[pl.BlockSpec(memory_space=space) for space in in_spaces],
        out_specs=[pl.BlockSpec(memory_space=space) for space in out_spaces],
        out_shape=[colour[space](s.shape, s.dtype) if space in colour else s for space, s in outs],
        scratch_shapes=[VMEM(s.shape, s.dtype) for s in scratch]
        + [pltpu.SemaphoreType.DMA((copies,))],
        input_output_aliases=aliases,
        compiler_params=pltpu.CompilerParams(vmem_limit_bytes=megabytes * 2**20),
        cost_estimate=pl.CostEstimate(
            flops=int(2e9 * gmacs), bytes_accessed=2**20, transcendentals=0
        ),
    )(*arrays)


ROWS = shape(LEN, D)
WIDE = shape(LEN, D, dtype=f32)
TALL = shape(D, LEN)
SPREAD = shape(LEN, FF)
RANKED = shape(LEN, RANK)
LOWER = shape(RANK, D)
UPPER = shape(D, RANK)
QKV = shape(3, D, D)
OUT = shape(D, D)
UP = shape(D, FF)
DOWN = shape(FF, D)
EXPON = shape(HEADS, LEN, LEN)
PER_HEAD = shape(16, LEN, dtype=f32)
SCORE = shape(2, LEN, LEN, dtype=f32)
SCORE_LOW = shape(2, LEN, LEN)
BIAS = shape(LEN, LEN, dtype=f32)
INV_STD = shape(LEN, 128, dtype=f32)
COLUMNS = shape(D, 16, dtype=f32)
RANKS = shape(2, RANK, dtype=f32)
SUMS = shape(4, RANK, dtype=f32)


def spread_sum(block, axis, first, last):
    size = lax.axis_size(axis)
    if size & (size - 1):
        return lax.psum(block, axis) if first == 0 else block
    for step in [1 << n for n in range(size.bit_length() - 1)][first:last]:
        block = block + lax.ppermute(block, axis, [(i, i ^ step) for i in range(size)])
    return block


def body(
    inputs, cotangent, pair_lengths, padding, qkv_weights, out_weights, up_weights, down_weights,
    layer_vectors, up_biases, shared_in, shared_out, scale_rank, scale_width,
):
    sec = lax.axis_index("section").astype(jnp.int32).reshape(1)

    def swap(block):
        return lax.ppermute(block, "section", [(0, 1), (1, 0)])

    def spaced(space, *arrays):
        return [(space, a) for a in arrays]

    small = (scale_rank, scale_width, layer_vectors, up_biases)
    large = (qkv_weights, out_weights, up_weights, down_weights)
    got_rank = swap(scale_rank)
    got_rank, small_now, large = lax.optimization_barrier((got_rank, small[1:], large))
    got_small = (got_rank,) + tuple(swap(block) for block in small_now)
    got_qkv, got_out = swap(large[0]), swap(large[1])
    lower = (HBM, shared_in)
    upper = (HBM, shared_out)
    sec = (SMEM, sec)
    lengths = (SMEM, pair_lengths)
    pads = (SMEM, padding.reshape(-1))

    ranks = [(HBM, scale_rank), (HELD, got_rank)]
    h, reduced, vera_q, vera_v = call(
        rank_kernel, "ranks", [sec, (HBM, inputs), lower, upper] + ranks,
        spaced(HELD, ROWS, RANKED, TALL, TALL),
        [LOWER, UPPER, RANKS, RANKS, RANKED, RANKED], 4, 1.2, 45,
    )
    got_small, got_qkv, got_out, rest, h = lax.optimization_barrier(
        (got_small, got_qkv, got_out, large[2:], h)
    )
    ranks, widths, vectors, biases = (
        spaced(HELD, own, other) for own, other in zip(small, got_small)
    )
    got_down, got_up = swap(rest[1]), swap(rest[0])
    *kept, inverse = call(
        attend_kernel, "attention",
        [sec, lengths, pads] + spaced(HELD, qkv_weights, got_qkv, out_weights, got_out)
        + vectors + widths + spaced(HELD, h, reduced, vera_q, vera_v),
        spaced(HBM, RANKED, TALL, TALL, TALL, TALL, TALL, EXPON, TALL, WIDE, ROWS, ROWS, INV_STD)
        + spaced(HELD, PER_HEAD),
        [QKV, OUT, TALL, TALL, TALL, EXPON, TALL, WIDE, ROWS, ROWS, INV_STD, BIAS, COLUMNS, SCORE],
        23, 2.8, 45,
    )
    qkv = spaced(HBM, qkv_weights, got_qkv)
    w_out = [(HBM, out_weights), (pl.ANY, got_out)]
    w_up = spaced(HBM, up_weights, got_up)
    w_down = spaced(HBM, down_weights, got_down)
    both = shape(1, *inputs.shape)
    operands = (
        [sec, lengths, pads, (HBM, cotangent), lower, upper]
        + qkv + w_out + w_up + w_down + vectors + biases + ranks + widths
    )
    keep_sums, send_sums, section_outputs, input_grads, send_output, send_grad, _ = call(
        main_kernel, "main",
        operands
        + spaced(HBM, *kept) + spaced(HELD, inverse),
        spaced(HELD, SUMS, SUMS) + spaced(HBM, both, both, ROWS, ROWS, SPREAD),
        [ROWS, ROWS, ROWS, LOWER, UPPER, QKV, OUT, UP, DOWN, RANKS, COLUMNS, RANKED,
         TALL, TALL, TALL, TALL, TALL, BIAS, SCORE, EXPON, PER_HEAD, TALL,
         ROWS, ROWS, INV_STD, ROWS, INV_STD, ROWS, INV_STD,
         TALL, PER_HEAD, SCORE_LOW, TALL, TALL, TALL, SUMS, SUMS, SPREAD, SPREAD, WIDE, ROWS, INV_STD],
        48, 22.0, 60,
    )
    sums = keep_sums + swap(send_sums)
    got_output, got_grad = swap(send_output), swap(send_grad)
    sums = spread_sum(sums, "dp", 0, 1)
    section_outputs, input_grads = call(
        finish_kernel, "finish",
        [sec] + spaced(HELD, got_output, got_grad) + spaced(HBM, section_outputs, input_grads),
        spaced(HBM, both, both), [], 2, 0.1, 8, {3: 0, 4: 1},
    )
    sums, section_outputs, input_grads = lax.optimization_barrier(
        (sums, section_outputs, input_grads)
    )
    sums = spread_sum(sums, "dp", 1, None)
    return section_outputs, input_grads, sums[None, :2], sums[None, 2:, :D]


def solution(mesh):
    in_specs = (
        P(None, "dp", None, None),
        P(None, "dp", None, None),
        P(None, "dp", None),
        P(None, "dp"),
        P("section", None, None, None),
        P("section", None, None),
        P("section", None, None),
        P("section", None, None),
        P("section", None, None),
        P("section", None),
        P(),
        P(),
        P("section", None, None),
        P("section", None, None),
    )
    out_specs = (
        P("section", None, "dp", None, None),
        P("section", None, "dp", None, None),
        P("section", None, None),
        P("section", None, None),
    )
    return jax.shard_map(body, mesh=mesh, in_specs=in_specs, out_specs=out_specs, check_vma=False)
```

```python
import jax
import jax.numpy as jnp
from jax import lax
from jax.experimental import pallas as pl
from jax.experimental.pallas import tpu as pltpu
from jax.sharding import PartitionSpec as P

D = 768
HEADS = 12
HEAD_DIM = 64
FF = 3072
RANK = 1024
LEN = 512
CUT = 256
ROW_CUT = 128

epsilon = 1e-05
bf16 = jnp.bfloat16
f32 = jnp.float32

HBM = pltpu.HBM
VMEM = pltpu.VMEM
SMEM = pltpu.SMEM


def dg(left, right, left_dim, right_dim):
    return lax.dot_general(
        left, right, (((left_dim,), (right_dim,)), ((), ())), preferred_element_type=f32
    )


def head_rows(head):
    return slice(HEAD_DIM * head, HEAD_DIM * (head + 1))


def cuts(total, size):
    return [slice(start, start + size) for start in range(0, total, size)]


def fill_bias(bias, lengths, padding, seq):
    bounds = []
    total = 0
    for j in range(lengths.shape[2] - 1):
        total = total + lengths[seq, 0, j]
        bounds.append(total)
    key_pos = lax.broadcasted_iota(jnp.int32, (LEN, 1), 0)
    query_pos = lax.broadcasted_iota(jnp.int32, (1, LEN), 1)
    key_doc = sum((key_pos >= b).astype(jnp.int32) for b in bounds)
    query_doc = sum((query_pos >= b).astype(jnp.int32) for b in bounds)
    key_doc = jnp.where(key_pos < LEN - padding[seq], key_doc, -1)
    seen = (key_doc == query_doc) | (key_pos == query_pos)
    bias[...] = jnp.where(seen, 0.0, -1e30)


def norm_rows(values):
    average = jnp.mean(values, axis=-1, keepdims=True)
    centered = values - average
    variance = jnp.mean(centered * centered, axis=-1, keepdims=True)
    inv_std = lax.rsqrt(variance + epsilon)
    return centered * inv_std, inv_std


def norm_back(normal, inv_std, scaled):
    return inv_std * (
        scaled
        - jnp.mean(scaled, axis=-1, keepdims=True)
        - normal * jnp.mean(scaled * normal, axis=-1, keepdims=True)
    )


def rank_lower(h, lower, ranks, reduced, rank_q, rank_v):
    for c in cuts(RANK, CUT):
        part = dg(h[...], lower[c, :], 1, 1)
        reduced[:, c] = part.astype(bf16)
        rank_q[:, c] = (ranks[0:1, c] * part).astype(bf16)
        rank_v[:, c] = (ranks[1:2, c] * part).astype(bf16)


def rank_upper(upper, rank, vera):
    for c in cuts(D, CUT):
        vera[c, :] = dg(upper[c, :], rank[...], 1, 1).astype(bf16)


def project_queries(h, weights, columns, vera, queries):
    for c in cuts(D, CUT):
        part = dg(weights[:, c], h[...], 0, 1)
        part = part + columns[c, 0:1] + columns[c, 8:9] * vera[c, :].astype(f32)
        queries[c, :] = part.astype(bf16) * jnp.asarray(HEAD_DIM**-0.5, bf16)


def project_keys(h, weights, keys):
    for c in cuts(D, CUT):
        keys[c, :] = dg(weights[:, c], h[...], 0, 1).astype(bf16)


def project_values(h, weights, columns, vera, values):
    for c in cuts(D, CUT):
        part = dg(weights[:, c], h[...], 0, 1)
        part = part + columns[c, 1:2] + columns[c, 9:10] * vera[c, :].astype(f32)
        values[c, :] = part.astype(bf16)


def attend(queries, keys, values, bias, score, expon, inverse, context, done=None):
    for t in range(HEADS + 2):
        if t < HEADS:
            r = head_rows(t)
            score[t % 2] = dg(keys[r, :], queries[r, :], 0, 0)
        if 0 <= t - 2:
            r = head_rows(t - 2)
            part = dg(values[r, :], expon(t - 2)[...], 1, 0) * inverse[t - 2 : t - 1, :]
            context[r, :] = part.astype(bf16)
        if 0 <= t - 1 < HEADS:
            masked = score[(t - 1) % 2] + bias[...]
            e = jnp.exp(masked - jnp.max(masked, axis=0, keepdims=True))
            inverse[t - 1 : t, :] = 1.0 / jnp.sum(e, axis=0, keepdims=True)
            expon(t - 1)[...] = e.astype(bf16)
            if done is not None:
                done(t - 1)


def staged(size, first, second):
    blocks = cuts(LEN, size)
    for n in range(len(blocks) + 1):
        if n < len(blocks):
            first(blocks[n], n % 2)
        if n > 0:
            second(blocks[n - 1], (n - 1) % 2)


def first_norm(h, context, w_out, vectors, normed, normed_low, normal, inv_std, buffer):
    def product(c, slot):
        total = dg(context[:, c], w_out[...], 0, 0) + h[c, :].astype(f32)
        buffer[slot, : c.stop - c.start] = total + vectors[2:3, :]

    def norm(c, slot):
        xhat, s = norm_rows(buffer[slot, : c.stop - c.start])
        normal[c, :] = xhat.astype(bf16)
        inv_std[c, :] = jnp.broadcast_to(s, (c.stop - c.start, 128))
        out = xhat * vectors[3:4, :] + vectors[4:5, :]
        normed[c, :] = out
        normed_low[c, :] = out.astype(bf16)

    staged(ROW_CUT, product, norm)


def widen(normed_low, w_up, up_bias, active, slope, part):
    for start in range(part.start, part.stop, CUT):
        c = slice(start, start + CUT)
        x = dg(normed_low[...], w_up[:, c], 1, 0) + up_bias[:, c]
        share = 0.5 + 0.5 * lax.erf(x * 0.7071067811865476)
        active[:, c] = (x * share).astype(bf16)
        bell = jnp.exp(x * x * -0.5) * 0.3989422804014327
        slope[:, c] = (share + x * bell).astype(bf16)


def narrow(active, w_down, vectors, normed, result, normal, inv_std, buffer, after=None):
    def product(c, slot):
        total = dg(active[c, :], w_down[...], 1, 0) + normed[c, :]
        buffer[slot, : c.stop - c.start] = total + vectors[5:6, :]

    def norm(c, slot):
        xhat, s = norm_rows(buffer[slot, : c.stop - c.start])
        normal[c, :] = xhat.astype(bf16)
        inv_std[c, :] = jnp.broadcast_to(s, (c.stop - c.start, 128))
        result[c, :] = (xhat * vectors[6:7, :] + vectors[7:8, :]).astype(bf16)
        if after is not None:
            after(c)

    staged(ROW_CUT, product, norm)


def second_back(g, vectors, normal, inv_std, wide, low, c):
    scaled = g[c, :].astype(f32) * vectors[6:7, :]
    out = norm_back(normal[c, :].astype(f32), inv_std[c, 0:1], scaled)
    wide[c, :] = out
    low[c, :] = out.astype(bf16)


def feed_back(low, w_down, slope, grad_before):
    for c in cuts(FF, 2 * CUT):
        part = dg(low[...], w_down[c, :], 1, 1)
        grad_before[:, c] = (part * slope[:, c].astype(f32)).astype(bf16)


def first_back(grad_before, w_up, vectors, normal, inv_std, wide, low, buffer):
    def product(c, slot):
        buffer[slot, : c.stop - c.start] = dg(grad_before[c, :], w_up[...], 1, 1) + wide[c, :]

    def norm(c, slot):
        scaled = buffer[slot, : c.stop - c.start] * vectors[3:4, :]
        out = norm_back(normal[c, :].astype(f32), inv_std[c, 0:1], scaled)
        wide[c, :] = out
        low[c, :] = out.astype(bf16)

    staged(CUT, product, norm)


def context_back(low, w_out, inverse, context, grad_context, delta):
    for c in cuts(D, CUT):
        part = dg(w_out[c, :], low[...], 1, 1)
        for n in range(CUT // HEAD_DIM):
            head = c.start // HEAD_DIM + n
            r = head_rows(head)
            own = (part[head_rows(n), :] * inverse[head : head + 1, :]).astype(bf16)
            grad_context[r, :] = own
            delta[head : head + 1, :] = jnp.sum(
                own.astype(f32) * context[r, :].astype(f32), axis=0, keepdims=True
            )


def attend_back(
    queries, keys, values, expon, grad_context, delta, score, grad_score, grad_q, grad_k, grad_v,
    columns, vera_q, vera_v,
):
    for t in range(HEADS + 2):
        if t < HEADS:
            r = head_rows(t)
            score[t % 2] = dg(values[r, :], grad_context[r, :], 0, 0)
        if 0 <= t - 2:
            r = head_rows(t - 2)
            own = grad_score.at[t % 2]
            grad_q[r, :] = (dg(keys[r, :], own[...], 1, 0) * HEAD_DIM**-0.5).astype(bf16)
            grad_v[r, :] = dg(grad_context[r, :], expon(t - 2)[...], 1, 1).astype(bf16)
            grad_k[r, :] = dg(queries[r, :], own[...], 1, 1).astype(bf16)
        if 0 <= t - 1 < HEADS:
            part = score[(t - 1) % 2] - delta[t - 1 : t, :]
            grad_score[(t - 1) % 2] = (expon(t - 1)[...].astype(f32) * part).astype(bf16)


def rank_back(
    grad_q, grad_v, columns, upper, ranks, reduced, vera_q, vera_v, grad_reduced, sums
):
    for grad, vera, column in ((grad_q, vera_q, 8), (grad_v, vera_v, 9)):
        wide = grad[...].astype(f32)
        columns[:, column + 2 : column + 3] = jnp.sum(
            vera[...].astype(f32) * wide, axis=1, keepdims=True
        )
        vera[...] = (columns[:, column : column + 1] * wide).astype(bf16)
    turned = jnp.transpose(columns[...])
    sums[2:4, :D] = turned[10:12, :]
    sums[2:4, D:] = jnp.zeros((2, RANK - D), f32)
    for c in cuts(RANK, CUT):
        part_q = dg(vera_q[...], upper[:, c], 0, 0)
        part_v = dg(vera_v[...], upper[:, c], 0, 0)
        own = reduced[:, c].astype(f32)
        sums[0:1, c] = jnp.sum(own * part_q, axis=0, keepdims=True)
        sums[1:2, c] = jnp.sum(own * part_v, axis=0, keepdims=True)
        grad_reduced[:, c] = (ranks[0:1, c] * part_q + ranks[1:2, c] * part_v).astype(bf16)


def input_back(
    wide, grad_q, grad_k, grad_v, grad_reduced, w_q, w_k, w_v, lower, result, after=None
):
    def product(c, slot):
        total = wide[c, :] + dg(grad_q[:, c], w_q[...], 0, 1)
        total = total + dg(grad_k[:, c], w_k[...], 0, 1)
        total = total + dg(grad_v[:, c], w_v[...], 0, 1)
        total = total + dg(grad_reduced[c, :], lower[...], 1, 0)
        result[c, :] = total.astype(bf16)

    staged(CUT, product, lambda c, slot: after(c) if after is not None else None)


class Copies:
    def __init__(self, sems):
        self.sems = sems
        self.count = 0

    def start(self, source, target):
        copy = pltpu.make_async_copy(source, target, self.sems.at[self.count])
        self.count += 1
        copy.start()
        return copy

    def pick(self, condition, one, other):
        sem = self.sems.at[self.count]
        self.count += 1

        @pl.when(condition)
        def _():
            pltpu.make_async_copy(*one, sem).start()

        @pl.when(jnp.logical_not(condition))
        def _():
            pltpu.make_async_copy(*other, sem).start()

        return pltpu.make_async_copy(*one, sem)

    def load(self, condition, pair, index, target):
        return self.pick(condition, (pair[0].at[index], target), (pair[1].at[index], target))


def wait(*copies):
    for copy in copies:
        copy.wait()


def choose(condition, pair):
    return jnp.where(condition, pair[0][0], pair[1][0])


def make_columns(vectors, widths):
    rows = jnp.concatenate([vectors, widths, jnp.zeros((6, D), f32)], axis=0)
    return jnp.transpose(rows)


def reduce_kernel(sec, inputs, lower, h, reduced, low_v, sems):
    copies = Copies(sems)
    wait(copies.start(inputs.at[sec[0], 0], h), copies.start(lower, low_v))
    for c in cuts(RANK, CUT):
        reduced[:, c] = dg(h[...], low_v[c, :], 1, 1)


def attend_kernel(
    sec, lengths, padding, qkv_own, qkv_got, out_own, out_got, vec_own, vec_got, width_own, width_got,
    ranks_own, ranks_got, h, reduced_wide, upper,
    reduced_out, vera_q_out, vera_v_out, queries_out, keys_out, values_out, expon_out,
    context_out, normed_out, normed_low_out, normal_out, inv_std_out, inverse_out,
    qkv, w_out, queries, keys, values, expon, context, normed, normed_low, normal, inv_std,
    bias, columns, score, buffer, inverse, up_v, reduced, rank_q, rank_v, vera_q, vera_v, sems,
):
    seq = sec[0]
    copies = Copies(sems)
    mine = seq == 0
    vectors = choose(mine, (vec_own, vec_got))
    wait_upper = copies.start(upper, up_v)
    wait_qkv = [copies.load(mine, (qkv_own, qkv_got), (0, n), qkv.at[n]) for n in (1, 0, 2)]
    ranks = choose(mine, (ranks_own, ranks_got))
    for c in cuts(RANK, CUT):
        part = reduced_wide[:, c]
        reduced[:, c] = part.astype(bf16)
        rank_q[:, c] = (ranks[0:1, c] * part).astype(bf16)
        rank_v[:, c] = (ranks[1:2, c] * part).astype(bf16)
    columns[...] = make_columns(vectors, choose(mine, (width_own, width_got)))
    fill_bias(bias, lengths, padding, seq)
    wait(wait_upper)
    rank_upper(up_v, rank_q, vera_q)
    rank_upper(up_v, rank_v, vera_v)
    wait(*wait_qkv)
    project_keys(h, qkv.at[1], keys)
    outs = [
        copies.start(keys, keys_out),
        copies.start(reduced, reduced_out),
        copies.start(vera_q, vera_q_out),
        copies.start(vera_v, vera_v_out),
    ]
    project_queries(h, qkv.at[0], columns, vera_q, queries)
    outs.append(copies.start(queries, queries_out))
    project_values(h, qkv.at[2], columns, vera_v, values)
    outs.append(copies.start(values, values_out))

    def block(head):
        return expon.at[head]

    def done(head):
        outs.append(copies.start(expon.at[head], expon_out.at[head]))

    attend(queries, keys, values, bias, score, block, inverse, context, done)
    outs.append(copies.start(context, context_out))
    outs.append(copies.start(inverse, inverse_out))
    w_out[...] = jnp.where(mine, out_own[0], out_got[0])
    first_norm(h, context, w_out, vectors, normed, normed_low, normal, inv_std, buffer)
    outs += [
        copies.start(normed_low, normed_low_out),
        copies.start(normed, normed_out),
        copies.start(normal, normal_out),
        copies.start(inv_std, inv_std_out),
    ]
    wait(*outs)


def main_kernel(
    sec, lengths, padding, cotangent, lower, upper,
    qkv_own, qkv_got, out_own, out_got, up_own, up_got, down_own, down_got,
    vec_own, vec_got, bias_own, bias_got, ranks_own, ranks_got, width_own, width_got,
    reduced_0, vera_q_0, vera_v_0, queries_0, keys_0, values_0, expon_0,
    context_0, normed_0, normed_low_0, normal_0, inv_std_0, inverse_0,
    keep_sums, send_sums, keep_grad, send_grad,
    section_outputs, send_output, slope_0,
    h, g, second, low_v, up_v, qkv, w_out, w_up, w_down, ranks, columns, reduced,
    vera_q, vera_v, queries, keys, values, bias, score, expon_v, inverse, context,
    low, normal_1, inv_std_1, normal_2, inv_std_2, first_2, first_2s,
    grad_context, delta, grad_score, grad_q, grad_k, grad_v, sums_0, sums_1, active, slope, wide,
    first_1, first_1s, buffer, vec_v, bias_v, ranks_v, width_v, sems,
):
    seq = sec[0]
    leading = seq == 0
    following = seq == 1
    copies = Copies(sems)
    w_qkv, w_o, w_u, w_d = (
        (qkv_own, qkv_got), (out_own, out_got), (up_own, up_got), (down_own, down_got),
    )
    wait_small = []
    pairs = []
    for own, other, place in (
        (vec_own, vec_got, vec_v),
        (bias_own, bias_got, bias_v),
        (ranks_own, ranks_got, ranks_v),
        (width_own, width_got, width_v),
    ):
        blocks = place.at[0:1], place.at[1:2]
        if place is bias_v:
            blocks = place.at[0], place.at[1]
        wait_small += [copies.start(own, blocks[0]), copies.start(other, blocks[1])]
        pairs.append(blocks)
    vecs, biases, rank_pair, width_pair = pairs
    w_q, w_k, w_v = qkv.at[0], qkv.at[1], qkv.at[2]
    rank_q, rank_v = active.at[:, 0:RANK], active.at[:, RANK : 2 * RANK]

    def expon(head):
        return expon_v.at[head]

    parts = cuts(FF, FF // 4)

    def load_up(c):
        return copies.pick(
            leading, (up_own.at[0, :, c], w_up.at[:, c]), (up_got.at[0, :, c], w_up.at[:, c])
        )

    def load_down(c):
        return copies.pick(
            leading, (down_own.at[0, c], w_down.at[c]), (down_got.at[0, c], w_down.at[c])
        )

    wait_low = copies.start(normed_low_0, low)
    wait_ups = [load_up(c) for c in parts[:3]]
    wait(*wait_small)
    vectors = choose(leading, vecs)
    up_bias = jnp.where(leading, biases[0][...], biases[1][...])
    fill_bias(bias, lengths, padding, seq)
    wait(wait_low)
    outs = []
    for n, c in enumerate(parts):
        wait(wait_ups[n])
        if n == 0:
            wait_ups.append(load_up(parts[3]))
            wait_down = [load_down(c) for c in parts]
            wait_normed = copies.start(normed_0, wide)
        if n == 2:
            wait_lower = copies.start(lower, low_v)
            wait_upper = copies.start(upper, up_v)
        widen(low, w_up, up_bias, active, slope, c)
        outs.append(copies.start(slope.at[:, c], slope_0.at[:, c]))
    wait(wait_normed, *wait_down)
    wait_up = copies.load(following, w_u, 0, w_up)
    wait_qkv = [copies.load(following, w_qkv, (0, n), qkv.at[n]) for n in range(3)]
    narrow(active, w_down, vectors, wide, h, first_2, first_2s, buffer)
    out_first = copies.pick(
        leading, (h, section_outputs.at[0, 0, 0]), (h, send_output)
    )

    vectors = choose(following, vecs)
    up_bias = jnp.where(following, biases[0][...], biases[1][...])
    columns[...] = make_columns(vectors, choose(following, width_pair))
    ranks[...] = choose(following, rank_pair)
    wait(wait_lower)
    rank_lower(h, low_v, ranks, reduced, rank_q, rank_v)
    wait(wait_upper)
    rank_upper(up_v, rank_q, vera_q)
    rank_upper(up_v, rank_v, vera_v)
    wait_out = copies.load(following, w_o, 0, w_out)
    wait_down = copies.load(following, w_d, 0, w_down)
    wait_g = copies.start(cotangent.at[seq, 0], g)
    wait_first = [copies.start(normal_0, first_1), copies.start(inv_std_0, first_1s)]
    wait(*wait_qkv)
    project_keys(h, w_k, keys)
    project_queries(h, w_q, columns, vera_q, queries)
    project_values(h, w_v, columns, vera_v, values)
    attend(queries, keys, values, bias, score, expon, inverse, context)
    wait(wait_out)
    first_norm(h, context, w_out, vectors, wide, low, normal_1, inv_std_1, buffer)
    wait(wait_up, *outs)
    for c in parts:
        widen(low, w_up, up_bias, active, slope, c)
    wait(wait_down, wait_g)

    def last_back(c):
        second_back(g, vectors, normal_2, inv_std_2, wide, low, c)

    narrow(active, w_down, vectors, wide, second, normal_2, inv_std_2, buffer, last_back)
    out_second = copies.pick(
        following, (second, section_outputs.at[0, 1, 0]), (second, send_output)
    )

    feed_back(low, w_down, slope, active)
    wait_down = copies.load(leading, w_d, 0, w_down)
    wait_slope = copies.start(slope_0, slope)
    first_back(active, w_up, vectors, normal_1, inv_std_1, wide, low, buffer)
    wait_up = copies.load(leading, w_u, 0, w_up)
    context_back(low, w_out, inverse, context, grad_context, delta)
    wait_out = copies.load(leading, w_o, 0, w_out)
    wait_context = [copies.start(context_0, context), copies.start(inverse_0, inverse)]
    attend_back(
        queries, keys, values, expon, grad_context, delta, score, grad_score, grad_q, grad_k, grad_v,
        columns, vera_q, vera_v,
    )
    wait_attend = [
        copies.start(values_0, values),
        copies.start(expon_0, expon_v),
        copies.start(keys_0, keys),
        copies.start(queries_0, queries),
    ]
    rank_back(grad_q, grad_v, columns, up_v, ranks, reduced, vera_q, vera_v, rank_q, sums_1)
    wait_ranks = [
        copies.start(reduced_0, reduced),
        copies.start(vera_q_0, vera_q),
        copies.start(vera_v_0, vera_v),
    ]
    vectors = choose(leading, vecs)

    def next_back(c):
        second_back(g, vectors, first_2, first_2s, wide, low, c)

    input_back(wide, grad_q, grad_k, grad_v, rank_q, w_q, w_k, w_v, low_v, g, next_back)
    wait_qkv = [copies.load(leading, w_qkv, (0, n), qkv.at[n]) for n in range(3)]

    columns[...] = make_columns(vectors, choose(leading, width_pair))
    ranks[...] = choose(leading, rank_pair)
    wait(wait_down, wait_slope)
    feed_back(low, w_down, slope, active)
    wait(wait_up, *wait_first)
    first_back(active, w_up, vectors, first_1, first_1s, wide, low, buffer)
    wait(wait_out, *wait_context)
    context_back(low, w_out, inverse, context, grad_context, delta)
    wait(*wait_attend, *wait_ranks)
    attend_back(
        queries, keys, values, expon, grad_context, delta, score, grad_score, grad_q, grad_k, grad_v,
        columns, vera_q, vera_v,
    )
    rank_back(grad_q, grad_v, columns, up_v, ranks, reduced, vera_q, vera_v, rank_q, sums_0)
    wait(*wait_qkv, out_second)
    input_back(wide, grad_q, grad_k, grad_v, rank_q, w_q, w_k, w_v, low_v, second)
    keep_grad[...] = jnp.where(leading, second[...], g[...])
    send_grad[...] = jnp.where(leading, g[...], second[...])
    keep_sums[...] = jnp.where(leading, sums_0[...], sums_1[...])
    send_sums[...] = jnp.where(leading, sums_1[...], sums_0[...])
    wait(out_first)


def finish_kernel(
    sec, got_output, keep_grad, got_grad, section_outputs, outputs_out, grads_out, sems
):
    own = sec[0]
    copies = Copies(sems)
    wait(
        copies.start(got_output, outputs_out.at[0, 1 - own, 0]),
        copies.start(keep_grad, grads_out.at[0, own, 0]),
        copies.start(got_grad, grads_out.at[0, 1 - own, 0]),
    )


def shape(*dims, dtype=bf16):
    return jax.ShapeDtypeStruct(dims, dtype)


HELD = "held"


def call(kernel, name, operands, outs, scratch, copies, gmacs, megabytes, aliases={}):
    in_spaces = [VMEM if space is HELD else space for space, _ in operands]
    out_spaces = [VMEM if space is HELD else space for space, _ in outs]
    colour = {HELD: VMEM, HBM: HBM}
    arrays = [
        pltpu.with_memory_space_constraint(array, colour[space]) if space in colour else array
        for space, array in operands
    ]
    return pl.pallas_call(
        kernel,
        name=name,
        in_specs=[pl.BlockSpec(memory_space=space) for space in in_spaces],
        out_specs=[pl.BlockSpec(memory_space=space) for space in out_spaces],
        out_shape=[colour[space](s.shape, s.dtype) if space in colour else s for space, s in outs],
        scratch_shapes=[VMEM(s.shape, s.dtype) for s in scratch]
        + [pltpu.SemaphoreType.DMA((copies,))],
        input_output_aliases=aliases,
        compiler_params=pltpu.CompilerParams(vmem_limit_bytes=megabytes * 2**20),
        cost_estimate=pl.CostEstimate(
            flops=int(2e9 * gmacs), bytes_accessed=2**20, transcendentals=0
        ),
    )(*arrays)


ROWS = shape(LEN, D)
WIDE = shape(LEN, D, dtype=f32)
TALL = shape(D, LEN)
SPREAD = shape(LEN, FF)
RANKED = shape(LEN, RANK)
LOWER = shape(RANK, D)
UPPER = shape(D, RANK)
QKV = shape(3, D, D)
OUT = shape(D, D)
UP = shape(D, FF)
DOWN = shape(FF, D)
EXPON = shape(HEADS, LEN, LEN)
PER_HEAD = shape(16, LEN, dtype=f32)
SCORE = shape(2, LEN, LEN, dtype=f32)
SCORE_LOW = shape(2, LEN, LEN)
BIAS = shape(LEN, LEN, dtype=f32)
INV_STD = shape(LEN, 128, dtype=f32)
COLUMNS = shape(D, 16, dtype=f32)
RANKS = shape(2, RANK, dtype=f32)
SUMS = shape(4, RANK, dtype=f32)
BUFFER = shape(2, CUT, D, dtype=f32)


def spread_sum(block, axis, first, last):
    size = lax.axis_size(axis)
    if size & (size - 1):
        return lax.psum(block, axis) if first == 0 else block
    for step in [1 << n for n in range(size.bit_length() - 1)][first:last]:
        block = block + lax.ppermute(block, axis, [(i, i ^ step) for i in range(size)])
    return block


def body(
    inputs, cotangent, pair_lengths, padding, qkv_weights, out_weights, up_weights, down_weights,
    layer_vectors, up_biases, shared_in, shared_out, scale_rank, scale_width,
):
    sec = lax.axis_index("section").astype(jnp.int32).reshape(1)

    def swap(block):
        return lax.ppermute(block, "section", [(0, 1), (1, 0)])

    def spaced(space, *arrays):
        return [(space, a) for a in arrays]

    small = (scale_rank, scale_width, layer_vectors, up_biases)
    large = (qkv_weights, out_weights, up_weights, down_weights, up_biases)
    got_small = tuple(swap(block) for block in small[:3])
    got_qkv, got_out = swap(large[0]), swap(large[1])
    lower = (HBM, shared_in)
    upper = (HBM, shared_out)
    sec = (SMEM, sec)
    lengths = (SMEM, pair_lengths)
    pads = (SMEM, padding.reshape(-1))

    h, reduced = call(
        reduce_kernel, "reduce", [sec, (HBM, inputs), lower],
        spaced(HELD, ROWS, shape(LEN, RANK, dtype=f32)), [LOWER], 2, 0.4, 48,
    )
    got_small, got_qkv, got_out, rest, h = lax.optimization_barrier(
        (got_small, got_qkv, got_out, large[2:], h)
    )
    ranks, widths, vectors = zip(small, got_small)
    biases = (up_biases, swap(rest[2]))
    got_down, got_up = swap(rest[1]), swap(rest[0])
    kept = call(
        attend_kernel, "attention",
        [sec, lengths, pads, (HBM, qkv_weights), (pl.ANY, got_qkv)]
        + spaced(HELD, out_weights, got_out)
        + spaced(HELD, *vectors, *widths, *ranks, h, reduced) + [upper],
        spaced(HBM, RANKED, TALL, TALL, TALL, TALL, TALL, EXPON, TALL, WIDE, ROWS, ROWS, INV_STD, PER_HEAD),
        [QKV, OUT, TALL, TALL, TALL, EXPON, TALL, WIDE, ROWS, ROWS, INV_STD, BIAS, COLUMNS, SCORE, BUFFER, PER_HEAD,
         UPPER, RANKED, RANKED, RANKED, TALL, TALL],
        28, 3.6, 48,
    )
    qkv = spaced(HBM, qkv_weights, got_qkv)
    w_out = [(HBM, out_weights), (pl.ANY, got_out)]
    w_up = spaced(HBM, up_weights, got_up)
    w_down = spaced(HBM, down_weights, got_down)
    both = shape(1, *inputs.shape)
    operands = (
        [sec, lengths, pads, (HBM, cotangent), lower, upper]
        + qkv + w_out + w_up + w_down
        + [pair for own, other in (vectors, biases, ranks, widths) for pair in ((HBM, own), (pl.ANY, other))]
    )
    keep_sums, send_sums, keep_grad, send_grad, section_outputs, send_output, _ = call(
        main_kernel, "main",
        operands
        + spaced(HBM, *kept),
        spaced(HELD, SUMS, SUMS, ROWS, ROWS) + spaced(HBM, both, ROWS, SPREAD),
        [ROWS, ROWS, ROWS, LOWER, UPPER, QKV, OUT, UP, DOWN, RANKS, COLUMNS, RANKED,
         TALL, TALL, TALL, TALL, TALL, BIAS, SCORE, EXPON, PER_HEAD, TALL,
         ROWS, ROWS, INV_STD, ROWS, INV_STD, ROWS, INV_STD,
         TALL, PER_HEAD, SCORE_LOW, TALL, TALL, TALL, SUMS, SUMS, SPREAD, SPREAD, WIDE, ROWS, INV_STD, BUFFER,
         shape(2, 8, D, dtype=f32), shape(2, 1, FF, dtype=f32), shape(2, 2, RANK, dtype=f32),
         shape(2, 2, D, dtype=f32)],
        57, 22.0, 60,
    )
    sums = keep_sums + swap(send_sums)
    sums, send_output, send_grad = lax.optimization_barrier((sums, send_output, send_grad))
    got_output, got_grad = swap(send_output), swap(send_grad)
    sums = spread_sum(sums, "dp", 0, -1)
    section_outputs, input_grads = call(
        finish_kernel, "finish",
        [sec] + spaced(HELD, got_output, keep_grad, got_grad) + spaced(HBM, section_outputs),
        spaced(HBM, both, both), [], 3, 2.0, 8, {4: 0},
    )
    sums, section_outputs, input_grads = lax.optimization_barrier(
        (sums, section_outputs, input_grads)
    )
    sums = spread_sum(sums, "dp", -1, None)
    return section_outputs, input_grads, sums[None, :2], sums[None, 2:, :D]


def solution(mesh):
    in_specs = (
        P(None, "dp", None, None),
        P(None, "dp", None, None),
        P(None, "dp", None),
        P(None, "dp"),
        P("section", None, None, None),
        P("section", None, None),
        P("section", None, None),
        P("section", None, None),
        P("section", None, None),
        P("section", None),
        P(),
        P(),
        P("section", None, None),
        P("section", None, None),
    )
    out_specs = (
        P("section", None, "dp", None, None),
        P("section", None, "dp", None, None),
        P("section", None, None),
        P("section", None, None),
    )
    return jax.shard_map(body, mesh=mesh, in_specs=in_specs, out_specs=out_specs, check_vma=False)
```

```python
import jax
import jax.numpy as jnp
from jax import lax
from jax.experimental import pallas as pl
from jax.experimental.pallas import tpu as pltpu
from jax.sharding import PartitionSpec as P

D = 768
HEADS = 12
HEAD_DIM = 64
FF = 3072
RANK = 1024
LEN = 512
CUT = 256
ROW_CUT = 128

epsilon = 1e-05
bf16 = jnp.bfloat16
f32 = jnp.float32

HBM = pltpu.HBM
VMEM = pltpu.VMEM
SMEM = pltpu.SMEM


def dg(left, right, left_dim, right_dim):
    return lax.dot_general(
        left, right, (((left_dim,), (right_dim,)), ((), ())), preferred_element_type=f32
    )


def head_rows(head):
    return slice(HEAD_DIM * head, HEAD_DIM * (head + 1))


def cuts(total, size):
    return [slice(start, start + size) for start in range(0, total, size)]


def fill_bias(bias, lengths, padding, seq):
    bounds = []
    total = 0
    for j in range(lengths.shape[2] - 1):
        total = total + lengths[seq, 0, j]
        bounds.append(total)
    key_pos = lax.broadcasted_iota(jnp.int32, (LEN, 1), 0)
    query_pos = lax.broadcasted_iota(jnp.int32, (1, LEN), 1)
    key_doc = sum((key_pos >= b).astype(jnp.int32) for b in bounds)
    query_doc = sum((query_pos >= b).astype(jnp.int32) for b in bounds)
    key_doc = jnp.where(key_pos < LEN - padding[seq], key_doc, -1)
    seen = (key_doc == query_doc) | (key_pos == query_pos)
    bias[...] = jnp.where(seen, 0.0, -1e30)


def norm_rows(values):
    average = jnp.mean(values, axis=-1, keepdims=True)
    centered = values - average
    variance = jnp.mean(centered * centered, axis=-1, keepdims=True)
    inv_std = lax.rsqrt(variance + epsilon)
    return centered * inv_std, inv_std


def norm_back(normal, inv_std, scaled):
    return inv_std * (
        scaled
        - jnp.mean(scaled, axis=-1, keepdims=True)
        - normal * jnp.mean(scaled * normal, axis=-1, keepdims=True)
    )


def rank_lower(h, lower, ranks, reduced, rank_q, rank_v):
    for c in cuts(RANK, CUT):
        part = dg(h[...], lower[c, :], 1, 1)
        reduced[:, c] = part.astype(bf16)
        rank_q[:, c] = (ranks[0:1, c] * part).astype(bf16)
        rank_v[:, c] = (ranks[1:2, c] * part).astype(bf16)


def rank_upper(upper, rank, vera):
    for c in cuts(D, CUT):
        vera[c, :] = dg(upper[c, :], rank[...], 1, 1).astype(bf16)


def project_queries(h, weights, columns, vera, queries):
    for c in cuts(D, CUT):
        part = dg(weights[:, c], h[...], 0, 1)
        part = part + columns[c, 0:1] + columns[c, 8:9] * vera[c, :].astype(f32)
        queries[c, :] = part.astype(bf16) * jnp.asarray(HEAD_DIM**-0.5, bf16)


def project_keys(h, weights, keys):
    for c in cuts(D, CUT):
        keys[c, :] = dg(weights[:, c], h[...], 0, 1).astype(bf16)


def project_values(h, weights, columns, vera, values):
    for c in cuts(D, CUT):
        part = dg(weights[:, c], h[...], 0, 1)
        part = part + columns[c, 1:2] + columns[c, 9:10] * vera[c, :].astype(f32)
        values[c, :] = part.astype(bf16)


def attend(queries, keys, values, bias, score, expon, inverse, context, done=None):
    for t in range(HEADS + 2):
        if t < HEADS:
            r = head_rows(t)
            score[t % 2] = dg(keys[r, :], queries[r, :], 0, 0)
        if 0 <= t - 2:
            r = head_rows(t - 2)
            part = dg(values[r, :], expon(t - 2)[...], 1, 0) * inverse[t - 2 : t - 1, :]
            context[r, :] = part.astype(bf16)
        if 0 <= t - 1 < HEADS:
            masked = score[(t - 1) % 2] + bias[...]
            e = jnp.exp(masked - jnp.max(masked, axis=0, keepdims=True))
            inverse[t - 1 : t, :] = 1.0 / jnp.sum(e, axis=0, keepdims=True)
            expon(t - 1)[...] = e.astype(bf16)
            if done is not None:
                done(t - 1)


def staged(size, first, second):
    blocks = cuts(LEN, size)
    for n in range(len(blocks) + 1):
        if n < len(blocks):
            first(blocks[n], n % 2)
        if n > 0:
            second(blocks[n - 1], (n - 1) % 2)


def first_norm(h, context, w_out, vectors, normed, normed_low, normal, inv_std, buffer):
    def product(c, slot):
        total = dg(context[:, c], w_out[...], 0, 0) + h[c, :].astype(f32)
        buffer[slot, : c.stop - c.start] = total + vectors[2:3, :]

    def norm(c, slot):
        xhat, s = norm_rows(buffer[slot, : c.stop - c.start])
        normal[c, :] = xhat.astype(bf16)
        inv_std[c, :] = jnp.broadcast_to(s, (c.stop - c.start, 128))
        out = xhat * vectors[3:4, :] + vectors[4:5, :]
        normed[c, :] = out
        normed_low[c, :] = out.astype(bf16)

    staged(ROW_CUT, product, norm)


def widen(normed_low, w_up, up_bias, active, slope, part):
    for start in range(part.start, part.stop, CUT):
        c = slice(start, start + CUT)
        x = dg(normed_low[...], w_up[:, c], 1, 0) + up_bias[:, c]
        share = 0.5 + 0.5 * lax.erf(x * 0.7071067811865476)
        active[:, c] = (x * share).astype(bf16)
        bell = jnp.exp(x * x * -0.5) * 0.3989422804014327
        slope[:, c] = (share + x * bell).astype(bf16)


def narrow(active, w_down, vectors, normed, result, normal, inv_std, buffer, after=None):
    def product(c, slot):
        total = dg(active[c, :], w_down[...], 1, 0) + normed[c, :]
        buffer[slot, : c.stop - c.start] = total + vectors[5:6, :]

    def norm(c, slot):
        xhat, s = norm_rows(buffer[slot, : c.stop - c.start])
        normal[c, :] = xhat.astype(bf16)
        inv_std[c, :] = jnp.broadcast_to(s, (c.stop - c.start, 128))
        result[c, :] = (xhat * vectors[6:7, :] + vectors[7:8, :]).astype(bf16)
        if after is not None:
            after(c)

    staged(ROW_CUT, product, norm)


def second_back(g, vectors, normal, inv_std, wide, low, c):
    scaled = g[c, :].astype(f32) * vectors[6:7, :]
    out = norm_back(normal[c, :].astype(f32), inv_std[c, 0:1], scaled)
    wide[c, :] = out
    low[c, :] = out.astype(bf16)


def feed_back(low, w_down, slope, grad_before):
    for c in cuts(FF, 2 * CUT):
        part = dg(low[...], w_down[c, :], 1, 1)
        grad_before[:, c] = (part * slope[:, c].astype(f32)).astype(bf16)


def first_back(grad_before, w_up, vectors, normal, inv_std, wide, low, buffer):
    def product(c, slot):
        buffer[slot, : c.stop - c.start] = dg(grad_before[c, :], w_up[...], 1, 1) + wide[c, :]

    def norm(c, slot):
        scaled = buffer[slot, : c.stop - c.start] * vectors[3:4, :]
        out = norm_back(normal[c, :].astype(f32), inv_std[c, 0:1], scaled)
        wide[c, :] = out
        low[c, :] = out.astype(bf16)

    staged(CUT, product, norm)


def context_back(low, w_out, inverse, context, grad_context, delta):
    for c in cuts(D, CUT):
        part = dg(w_out[c, :], low[...], 1, 1)
        for n in range(CUT // HEAD_DIM):
            head = c.start // HEAD_DIM + n
            r = head_rows(head)
            own = (part[head_rows(n), :] * inverse[head : head + 1, :]).astype(bf16)
            grad_context[r, :] = own
            delta[head : head + 1, :] = jnp.sum(
                own.astype(f32) * context[r, :].astype(f32), axis=0, keepdims=True
            )


def attend_back(
    queries, keys, values, expon, grad_context, delta, score, grad_score, grad_q, grad_k, grad_v,
    columns, vera_q, vera_v,
):
    for t in range(HEADS + 2):
        if t < HEADS:
            r = head_rows(t)
            score[t % 2] = dg(values[r, :], grad_context[r, :], 0, 0)
        if 0 <= t - 2:
            r = head_rows(t - 2)
            own = grad_score.at[t % 2]
            grad_q[r, :] = (dg(keys[r, :], own[...], 1, 0) * HEAD_DIM**-0.5).astype(bf16)
            grad_v[r, :] = dg(grad_context[r, :], expon(t - 2)[...], 1, 1).astype(bf16)
            grad_k[r, :] = dg(queries[r, :], own[...], 1, 1).astype(bf16)
        if 0 <= t - 1 < HEADS:
            part = score[(t - 1) % 2] - delta[t - 1 : t, :]
            grad_score[(t - 1) % 2] = (expon(t - 1)[...].astype(f32) * part).astype(bf16)


def rank_back(
    grad_q, grad_v, columns, upper, ranks, reduced, vera_q, vera_v, grad_reduced, sums
):
    for grad, vera, column in ((grad_q, vera_q, 8), (grad_v, vera_v, 9)):
        wide = grad[...].astype(f32)
        columns[:, column + 2 : column + 3] = jnp.sum(
            vera[...].astype(f32) * wide, axis=1, keepdims=True
        )
        vera[...] = (columns[:, column : column + 1] * wide).astype(bf16)
    turned = jnp.transpose(columns[...])
    sums[2:4, :D] = turned[10:12, :]
    sums[2:4, D:] = jnp.zeros((2, RANK - D), f32)
    for c in cuts(RANK, CUT):
        part_q = dg(vera_q[...], upper[:, c], 0, 0)
        part_v = dg(vera_v[...], upper[:, c], 0, 0)
        own = reduced[:, c].astype(f32)
        sums[0:1, c] = jnp.sum(own * part_q, axis=0, keepdims=True)
        sums[1:2, c] = jnp.sum(own * part_v, axis=0, keepdims=True)
        grad_reduced[:, c] = (ranks[0:1, c] * part_q + ranks[1:2, c] * part_v).astype(bf16)


def input_back(
    wide, grad_q, grad_k, grad_v, grad_reduced, w_q, w_k, w_v, lower, result, after=None
):
    def product(c, slot):
        total = wide[c, :] + dg(grad_q[:, c], w_q[...], 0, 1)
        total = total + dg(grad_k[:, c], w_k[...], 0, 1)
        total = total + dg(grad_v[:, c], w_v[...], 0, 1)
        total = total + dg(grad_reduced[c, :], lower[...], 1, 0)
        result[c, :] = total.astype(bf16)

    staged(CUT, product, lambda c, slot: after(c) if after is not None else None)


class Copies:
    def __init__(self, sems):
        self.sems = sems
        self.count = 0

    def start(self, source, target):
        copy = pltpu.make_async_copy(source, target, self.sems.at[self.count])
        self.count += 1
        copy.start()
        return copy

    def pick(self, condition, one, other):
        sem = self.sems.at[self.count]
        self.count += 1

        @pl.when(condition)
        def _():
            pltpu.make_async_copy(*one, sem).start()

        @pl.when(jnp.logical_not(condition))
        def _():
            pltpu.make_async_copy(*other, sem).start()

        return pltpu.make_async_copy(*one, sem)

    def load(self, condition, pair, index, target):
        return self.pick(condition, (pair[0].at[index], target), (pair[1].at[index], target))


def wait(*copies):
    for copy in copies:
        copy.wait()


def choose(condition, pair):
    return jnp.where(condition, pair[0][0], pair[1][0])


def make_columns(vectors, widths):
    rows = jnp.concatenate([vectors, widths, jnp.zeros((6, D), f32)], axis=0)
    return jnp.transpose(rows)


def reduce_kernel(sec, inputs, lower, h, reduced, low_v, sems):
    copies = Copies(sems)
    wait(copies.start(inputs.at[sec[0], 0], h), copies.start(lower, low_v))
    for c in cuts(RANK, CUT):
        reduced[:, c] = dg(h[...], low_v[c, :], 1, 1)


def attend_kernel(
    sec, lengths, padding, qkv_own, qkv_got, out_own, out_got, vec_own, vec_got, width_own, width_got,
    ranks_own, ranks_got, h, reduced_wide, upper,
    reduced_out, vera_q_out, vera_v_out, queries_out, keys_out, values_out, expon_out,
    context_out, normed_out, normed_low_out, normal_out, inv_std_out, inverse_out,
    qkv, w_out, queries, keys, values, expon, context, normed, normed_low, normal, inv_std,
    bias, columns, score, buffer, inverse, up_v, reduced, rank_q, rank_v, vera_q, vera_v, sems,
):
    seq = sec[0]
    copies = Copies(sems)
    mine = seq == 0
    vectors = choose(mine, (vec_own, vec_got))
    wait_upper = copies.start(upper, up_v)
    wait_qkv = [copies.load(mine, (qkv_own, qkv_got), (0, n), qkv.at[n]) for n in (1, 0, 2)]
    ranks = choose(mine, (ranks_own, ranks_got))
    for c in cuts(RANK, CUT):
        part = reduced_wide[:, c]
        reduced[:, c] = part.astype(bf16)
        rank_q[:, c] = (ranks[0:1, c] * part).astype(bf16)
        rank_v[:, c] = (ranks[1:2, c] * part).astype(bf16)
    columns[...] = make_columns(vectors, choose(mine, (width_own, width_got)))
    fill_bias(bias, lengths, padding, seq)
    wait(wait_upper)
    rank_upper(up_v, rank_q, vera_q)
    rank_upper(up_v, rank_v, vera_v)
    wait(*wait_qkv)
    wait_out = copies.load(mine, (out_own, out_got), 0, w_out)
    project_keys(h, qkv.at[1], keys)
    outs = [
        copies.start(keys, keys_out),
        copies.start(reduced, reduced_out),
        copies.start(vera_q, vera_q_out),
        copies.start(vera_v, vera_v_out),
    ]
    project_queries(h, qkv.at[0], columns, vera_q, queries)
    outs.append(copies.start(queries, queries_out))
    project_values(h, qkv.at[2], columns, vera_v, values)
    outs.append(copies.start(values, values_out))

    def block(head):
        return expon.at[head]

    def done(head):
        outs.append(copies.start(expon.at[head], expon_out.at[head]))

    attend(queries, keys, values, bias, score, block, inverse, context, done)
    outs.append(copies.start(context, context_out))
    outs.append(copies.start(inverse, inverse_out))
    wait(wait_out)
    first_norm(h, context, w_out, vectors, normed, normed_low, normal, inv_std, buffer)
    outs += [
        copies.start(normed_low, normed_low_out),
        copies.start(normed, normed_out),
        copies.start(normal, normal_out),
        copies.start(inv_std, inv_std_out),
    ]
    wait(*outs)


def main_kernel(
    sec, lengths, padding, cotangent, lower, upper,
    qkv_own, qkv_got, out_own, out_got, up_own, up_got, down_own, down_got,
    vec_own, vec_got, bias_own, bias_got, ranks_own, ranks_got, width_own, width_got,
    reduced_0, vera_q_0, vera_v_0, queries_0, keys_0, values_0, expon_0,
    context_0, normed_0, normed_low_0, normal_0, inv_std_0, inverse_0,
    keep_sums, send_sums, keep_grad, send_grad,
    section_outputs, send_output, slope_0,
    h, g, second, low_v, up_v, qkv, w_out, w_up, w_down, ranks, columns, reduced,
    vera_q, vera_v, queries, keys, values, bias, score, expon_v, inverse, context,
    low, normal_1, inv_std_1, normal_2, inv_std_2, first_2, first_2s,
    grad_context, delta, grad_score, grad_q, grad_k, grad_v, sums_0, sums_1, active, slope, wide,
    first_1, first_1s, buffer, vec_v, bias_v, ranks_v, width_v, sems,
):
    seq = sec[0]
    leading = seq == 0
    following = seq == 1
    copies = Copies(sems)
    w_qkv, w_o, w_u, w_d = (
        (qkv_own, qkv_got), (out_own, out_got), (up_own, up_got), (down_own, down_got),
    )
    wait_small = []
    pairs = []
    for own, other, place in (
        (vec_own, vec_got, vec_v),
        (bias_own, bias_got, bias_v),
        (ranks_own, ranks_got, ranks_v),
        (width_own, width_got, width_v),
    ):
        blocks = place.at[0:1], place.at[1:2]
        if place is bias_v:
            blocks = place.at[0], place.at[1]
        wait_small += [copies.start(own, blocks[0]), copies.start(other, blocks[1])]
        pairs.append(blocks)
    vecs, biases, rank_pair, width_pair = pairs
    w_q, w_k, w_v = qkv.at[0], qkv.at[1], qkv.at[2]
    rank_q, rank_v = active.at[:, 0:RANK], active.at[:, RANK : 2 * RANK]

    def expon(head):
        return expon_v.at[head]

    parts = cuts(FF, FF // 4)

    def load_up(c):
        return copies.pick(
            leading, (up_own.at[0, :, c], w_up.at[:, c]), (up_got.at[0, :, c], w_up.at[:, c])
        )

    def load_down(c):
        return copies.pick(
            leading, (down_own.at[0, c], w_down.at[c]), (down_got.at[0, c], w_down.at[c])
        )

    wait_low = copies.start(normed_low_0, low)
    wait_ups = [load_up(c) for c in parts[:3]]
    wait(*wait_small)
    vectors = choose(leading, vecs)
    up_bias = jnp.where(leading, biases[0][...], biases[1][...])
    fill_bias(bias, lengths, padding, seq)
    wait(wait_low)
    outs = []
    for n, c in enumerate(parts):
        wait(wait_ups[n])
        if n == 0:
            wait_ups.append(load_up(parts[3]))
            wait_down = [load_down(c) for c in parts]
            wait_normed = copies.start(normed_0, wide)
        if n == 2:
            wait_lower = copies.start(lower, low_v)
            wait_upper = copies.start(upper, up_v)
        widen(low, w_up, up_bias, active, slope, c)
        outs.append(copies.start(slope.at[:, c], slope_0.at[:, c]))
    wait(wait_normed, *wait_down)
    wait_up = copies.load(following, w_u, 0, w_up)
    wait_qkv = [copies.load(following, w_qkv, (0, n), qkv.at[n]) for n in range(3)]
    narrow(active, w_down, vectors, wide, h, first_2, first_2s, buffer)
    out_first = copies.pick(
        leading, (h, section_outputs.at[0, 0, 0]), (h, send_output)
    )

    vectors = choose(following, vecs)
    up_bias = jnp.where(following, biases[0][...], biases[1][...])
    columns[...] = make_columns(vectors, choose(following, width_pair))
    ranks[...] = choose(following, rank_pair)
    wait(wait_lower)
    rank_lower(h, low_v, ranks, reduced, rank_q, rank_v)
    wait(wait_upper)
    rank_upper(up_v, rank_q, vera_q)
    rank_upper(up_v, rank_v, vera_v)
    wait_out = copies.load(following, w_o, 0, w_out)
    wait_down = copies.load(following, w_d, 0, w_down)
    wait_g = copies.start(cotangent.at[seq, 0], g)
    wait_first = [copies.start(normal_0, first_1), copies.start(inv_std_0, first_1s)]
    wait(*wait_qkv)
    project_keys(h, w_k, keys)
    project_queries(h, w_q, columns, vera_q, queries)
    project_values(h, w_v, columns, vera_v, values)
    attend(queries, keys, values, bias, score, expon, inverse, context)
    wait(wait_out)
    first_norm(h, context, w_out, vectors, wide, low, normal_1, inv_std_1, buffer)
    wait(wait_up, *outs)
    for c in parts:
        widen(low, w_up, up_bias, active, slope, c)
    wait(wait_down, wait_g)

    def last_back(c):
        second_back(g, vectors, normal_2, inv_std_2, wide, low, c)

    narrow(active, w_down, vectors, wide, second, normal_2, inv_std_2, buffer, last_back)
    out_second = copies.pick(
        following, (second, section_outputs.at[0, 1, 0]), (second, send_output)
    )

    feed_back(low, w_down, slope, active)
    wait_down = copies.load(leading, w_d, 0, w_down)
    wait_slope = copies.start(slope_0, slope)
    first_back(active, w_up, vectors, normal_1, inv_std_1, wide, low, buffer)
    wait_up = copies.load(leading, w_u, 0, w_up)
    context_back(low, w_out, inverse, context, grad_context, delta)
    wait_out = copies.load(leading, w_o, 0, w_out)
    wait_context = [copies.start(context_0, context), copies.start(inverse_0, inverse)]
    attend_back(
        queries, keys, values, expon, grad_context, delta, score, grad_score, grad_q, grad_k, grad_v,
        columns, vera_q, vera_v,
    )
    wait_attend = [
        copies.start(values_0, values),
        copies.start(expon_0, expon_v),
        copies.start(keys_0, keys),
        copies.start(queries_0, queries),
    ]
    rank_back(grad_q, grad_v, columns, up_v, ranks, reduced, vera_q, vera_v, rank_q, sums_1)
    wait_ranks = [
        copies.start(reduced_0, reduced),
        copies.start(vera_q_0, vera_q),
        copies.start(vera_v_0, vera_v),
    ]
    vectors = choose(leading, vecs)

    def next_back(c):
        second_back(g, vectors, first_2, first_2s, wide, low, c)

    input_back(wide, grad_q, grad_k, grad_v, rank_q, w_q, w_k, w_v, low_v, g, next_back)
    wait_qkv = [copies.load(leading, w_qkv, (0, n), qkv.at[n]) for n in range(3)]

    columns[...] = make_columns(vectors, choose(leading, width_pair))
    ranks[...] = choose(leading, rank_pair)
    wait(wait_down, wait_slope)
    feed_back(low, w_down, slope, active)
    wait(wait_up, *wait_first)
    first_back(active, w_up, vectors, first_1, first_1s, wide, low, buffer)
    wait(wait_out, *wait_context)
    context_back(low, w_out, inverse, context, grad_context, delta)
    wait(*wait_attend, *wait_ranks)
    attend_back(
        queries, keys, values, expon, grad_context, delta, score, grad_score, grad_q, grad_k, grad_v,
        columns, vera_q, vera_v,
    )
    rank_back(grad_q, grad_v, columns, up_v, ranks, reduced, vera_q, vera_v, rank_q, sums_0)
    wait(*wait_qkv, out_second)
    input_back(wide, grad_q, grad_k, grad_v, rank_q, w_q, w_k, w_v, low_v, second)
    keep_grad[...] = jnp.where(leading, second[...], g[...])
    send_grad[...] = jnp.where(leading, g[...], second[...])
    keep_sums[...] = jnp.where(leading, sums_0[...], sums_1[...])
    send_sums[...] = jnp.where(leading, sums_1[...], sums_0[...])
    wait(out_first)


def finish_kernel(
    sec, got_output, keep_grad, got_grad, section_outputs, outputs_out, grads_out, sems
):
    own = sec[0]
    copies = Copies(sems)
    wait(
        copies.start(got_output, outputs_out.at[0, 1 - own, 0]),
        copies.start(keep_grad, grads_out.at[0, own, 0]),
        copies.start(got_grad, grads_out.at[0, 1 - own, 0]),
    )


def shape(*dims, dtype=bf16):
    return jax.ShapeDtypeStruct(dims, dtype)


HELD = "held"


def call(kernel, name, operands, outs, scratch, copies, gmacs, megabytes, aliases={}):
    in_spaces = [VMEM if space is HELD else space for space, _ in operands]
    out_spaces = [VMEM if space is HELD else space for space, _ in outs]
    colour = {HELD: VMEM, HBM: HBM}
    arrays = [
        pltpu.with_memory_space_constraint(array, colour[space]) if space in colour else array
        for space, array in operands
    ]
    return pl.pallas_call(
        kernel,
        name=name,
        in_specs=[pl.BlockSpec(memory_space=space) for space in in_spaces],
        out_specs=[pl.BlockSpec(memory_space=space) for space in out_spaces],
        out_shape=[colour[space](s.shape, s.dtype) if space in colour else s for space, s in outs],
        scratch_shapes=[VMEM(s.shape, s.dtype) for s in scratch]
        + [pltpu.SemaphoreType.DMA((copies,))],
        input_output_aliases=aliases,
        compiler_params=pltpu.CompilerParams(vmem_limit_bytes=megabytes * 2**20),
        cost_estimate=pl.CostEstimate(
            flops=int(2e9 * gmacs), bytes_accessed=2**20, transcendentals=0
        ),
    )(*arrays)


ROWS = shape(LEN, D)
WIDE = shape(LEN, D, dtype=f32)
TALL = shape(D, LEN)
SPREAD = shape(LEN, FF)
RANKED = shape(LEN, RANK)
LOWER = shape(RANK, D)
UPPER = shape(D, RANK)
QKV = shape(3, D, D)
OUT = shape(D, D)
UP = shape(D, FF)
DOWN = shape(FF, D)
EXPON = shape(HEADS, LEN, LEN)
PER_HEAD = shape(16, LEN, dtype=f32)
SCORE = shape(2, LEN, LEN, dtype=f32)
SCORE_LOW = shape(2, LEN, LEN)
BIAS = shape(LEN, LEN, dtype=f32)
INV_STD = shape(LEN, 128, dtype=f32)
COLUMNS = shape(D, 16, dtype=f32)
RANKS = shape(2, RANK, dtype=f32)
SUMS = shape(4, RANK, dtype=f32)
BUFFER = shape(2, CUT, D, dtype=f32)


def spread_sum(block, axis, first, last):
    size = lax.axis_size(axis)
    if size & (size - 1):
        return lax.psum(block, axis) if first == 0 else block
    for step in [1 << n for n in range(size.bit_length() - 1)][first:last]:
        block = block + lax.ppermute(block, axis, [(i, i ^ step) for i in range(size)])
    return block


def body(
    inputs, cotangent, pair_lengths, padding, qkv_weights, out_weights, up_weights, down_weights,
    layer_vectors, up_biases, shared_in, shared_out, scale_rank, scale_width,
):
    sec = lax.axis_index("section").astype(jnp.int32).reshape(1)

    def swap(block):
        return lax.ppermute(block, "section", [(0, 1), (1, 0)])

    def spaced(space, *arrays):
        return [(space, a) for a in arrays]

    small = (scale_rank, scale_width, layer_vectors, up_biases)
    large = (qkv_weights, out_weights, up_weights, down_weights, up_biases)
    got_small = tuple(swap(block) for block in small[:3])
    got_qkv, got_out = swap(large[0]), swap(large[1])
    lower = (HBM, shared_in)
    upper = (HBM, shared_out)
    sec = (SMEM, sec)
    lengths = (SMEM, pair_lengths)
    pads = (SMEM, padding.reshape(-1))

    h, reduced = call(
        reduce_kernel, "reduce", [sec, (HBM, inputs), lower],
        spaced(HELD, ROWS, shape(LEN, RANK, dtype=f32)), [LOWER], 2, 0.4, 59,
    )
    got_small, got_qkv, got_out, rest, h = lax.optimization_barrier(
        (got_small, got_qkv, got_out, large[2:], h)
    )
    ranks, widths, vectors = zip(small, got_small)
    biases = (up_biases, swap(rest[2]))
    got_down, got_up = swap(rest[1]), swap(rest[0])
    kept = call(
        attend_kernel, "attention",
        [sec, lengths, pads, (HBM, qkv_weights), (pl.ANY, got_qkv)]
        + [(HBM, out_weights), (pl.ANY, got_out)]
        + spaced(HELD, *vectors, *widths, *ranks, h, reduced) + [upper],
        spaced(HBM, RANKED, TALL, TALL, TALL, TALL, TALL, EXPON, TALL, WIDE, ROWS, ROWS, INV_STD, PER_HEAD),
        [QKV, OUT, TALL, TALL, TALL, EXPON, TALL, WIDE, ROWS, ROWS, INV_STD, BIAS, COLUMNS, SCORE, BUFFER, PER_HEAD,
         UPPER, RANKED, RANKED, RANKED, TALL, TALL],
        29, 3.6, 59,
    )
    qkv = spaced(HBM, qkv_weights, got_qkv)
    w_out = [(HBM, out_weights), (pl.ANY, got_out)]
    w_up = spaced(HBM, up_weights, got_up)
    w_down = spaced(HBM, down_weights, got_down)
    both = shape(1, *inputs.shape)
    operands = (
        [sec, lengths, pads, (HBM, cotangent), lower, upper]
        + qkv + w_out + w_up + w_down
        + [pair for own, other in (vectors, biases, ranks, widths) for pair in ((HBM, own), (pl.ANY, other))]
    )
    keep_sums, send_sums, keep_grad, send_grad, section_outputs, send_output, _ = call(
        main_kernel, "main",
        operands
        + spaced(HBM, *kept),
        spaced(HELD, SUMS, SUMS, ROWS, ROWS) + spaced(HBM, both, ROWS, SPREAD),
        [ROWS, ROWS, ROWS, LOWER, UPPER, QKV, OUT, UP, DOWN, RANKS, COLUMNS, RANKED,
         TALL, TALL, TALL, TALL, TALL, BIAS, SCORE, EXPON, PER_HEAD, TALL,
         ROWS, ROWS, INV_STD, ROWS, INV_STD, ROWS, INV_STD,
         TALL, PER_HEAD, SCORE_LOW, TALL, TALL, TALL, SUMS, SUMS, SPREAD, SPREAD, WIDE, ROWS, INV_STD, BUFFER,
         shape(2, 8, D, dtype=f32), shape(2, 1, FF, dtype=f32), shape(2, 2, RANK, dtype=f32),
         shape(2, 2, D, dtype=f32)],
        57, 22.0, 60,
    )
    sums = keep_sums + swap(send_sums)
    sums, send_output, send_grad = lax.optimization_barrier((sums, send_output, send_grad))
    got_output, got_grad = swap(send_output), swap(send_grad)
    sums = spread_sum(sums, "dp", 0, -1)
    section_outputs, input_grads = call(
        finish_kernel, "finish",
        [sec] + spaced(HELD, got_output, keep_grad, got_grad) + spaced(HBM, section_outputs),
        spaced(HBM, both, both), [], 3, 2.0, 8, {4: 0},
    )
    sums, section_outputs, input_grads = lax.optimization_barrier(
        (sums, section_outputs, input_grads)
    )
    sums = spread_sum(sums, "dp", -1, None)
    return section_outputs, input_grads, sums[None, :2], sums[None, 2:, :D]


def solution(mesh):
    in_specs = (
        P(None, "dp", None, None),
        P(None, "dp", None, None),
        P(None, "dp", None),
        P(None, "dp"),
        P("section", None, None, None),
        P("section", None, None),
        P("section", None, None),
        P("section", None, None),
        P("section", None, None),
        P("section", None),
        P(),
        P(),
        P("section", None, None),
        P("section", None, None),
    )
    out_specs = (
        P("section", None, "dp", None, None),
        P("section", None, "dp", None, None),
        P("section", None, None),
        P("section", None, None),
    )
    return jax.shard_map(body, mesh=mesh, in_specs=in_specs, out_specs=out_specs, check_vma=False)
```
